128 devices in a mesh: clu: 8 (over x, core), vol: 16 (over y, z).
Axes of the slice: x: 4, y: 4, z: 4, core: 2. Of those that a mesh axis runs over, the one named last changes fastest.
Arguments:
- volume_field: bfloat16 [16, 262144], P(None, ('clu', 'vol')), may hold values from -6 to 6
- trace_rows: int32 [1024, 128], P(('clu', 'vol')), may hold values from 0 to 262143, as said below
- near_block: bfloat16 [16384, 128, 128], P(('clu', 'vol')), may hold values from -0.125 to 0.125
- near_source: int32 [16384], P(('clu', 'vol')), may hold values from 0 to 7
- near_offset: int32 [16384], P(('clu', 'vol')), may hold values from 0 to 2
- near_cluster: int32 [16384], P(('clu', 'vol')), may hold values from 0 to 7
- far_v: bfloat16 [32768, 32, 128], P(('clu', 'vol')), may hold values from -0.5 to 0.5
- far_u: bfloat16 [32768, 32, 128], P(('clu', 'vol')), may hold values from -0.1875 to 0.1875
- far_source: int32 [32768], P(('clu', 'vol')), may hold values from 0 to 7
- far_owner: int32 [32768, 1], P(('clu', 'vol')), may hold values from 0 to 127; in each aligned block of 256 rows (0 to 255, 256 to 511, ...) at most 4 rows name the same one
- far_cluster: int32 [32768], P(('clu', 'vol')), may hold values from 0 to 7
Outputs:
- stray_trace: float32 [1024, 16, 128], P(('clu', 'vol'))
The draws below stay inside these ranges and needn't reach their ends.
Inputs may be any that keep to these rules, and one draw needn't show every extreme that they name: `trace_rows`: A node of cluster c reads a volume row r with r // 32768 == c // 128; the first and last row of each such range are read. `far_owner`: in the rows of one device (aligned blocks of 256 rows) no owner is named more than 4 times.
All inputs are finite; a program needn't handle non-finite values.
Results may differ from the reference program's by a relative error of at most 0.0021.
Values may be sent and summed in bfloat16 or wider, within the bound.
A program may use at most 64 MiB of HBM per device.

```python
import math
import jax
import jax.numpy as jnp
import numpy as np
from jax import lax

LEAF = 128
RANK = 32
NVEC = 16
NEAR_PER = 16
FAR_PER = 32
TC_DEV = 8
NCL = 1024
CL_GROUP = 128
NV = 262144
GROUP_ROWS = 32768
NP_DEV = 128
FP_DEV = 256
NPN = 16384
NPF = 32768
CAP = 4
DEVICES = 128


def draw_trace_rows(key, part):
    key = jax.random.fold_in(key, 7)
    picked = jax.random.randint(key, (NCL, LEAF), 0, GROUP_ROWS)
    node = jnp.arange(NCL * LEAF, dtype=jnp.int32).reshape(NCL, LEAF)
    group = node // (CL_GROUP * LEAF)
    within = node % (CL_GROUP * LEAF)
    picked = jnp.where(within == 0, 0, picked)
    picked = jnp.where(within == CL_GROUP * LEAF - 1, GROUP_ROWS - 1, picked)
    return (group * GROUP_ROWS + picked).astype(jnp.int32)


def touch_ends(entries, rng, smallest, largest):
    longest = entries.shape.index(max(entries.shape))
    spots = []
    for shift in (0, 1):
        where = [jax.random.randint(jax.random.fold_in(rng, axis), (), 0, length) for axis, length in enumerate(entries.shape)]
        where[longest] = (where[longest] + shift) % entries.shape[longest]
        spots.append(tuple(where))
    return entries.at[spots[0]].set(smallest).at[spots[1]].set(largest)


def block_scale(key, shape, split, least, top_value):
    loudness, own = 1.0, jax.random.fold_in(key, 6)
    for position, blocks in split:
        heights = jnp.exp(jax.random.uniform(jax.random.fold_in(own, position), (blocks,), jnp.float32, least / len(split), top_value / len(split)))
        loudness = loudness * jnp.repeat(heights, shape[position] // blocks).reshape([-1 if axis == position else 1 for axis in range(len(shape))])
    return loudness


def assign_block(key, own, number, rows, number_of, top, limit, lean):
    sequence = jax.random.permutation(key, number_of)
    heavy_load, common = load_shares(number_of, rows * top, limit, lean, True), load_shares(number_of, rows * top, limit, lean, False)
    places = jnp.arange(number_of)

    def named(tallies, turn):
        used = int((tallies > 0).sum())
        fixed = max(1, used // 4)
        moved = fixed + (places - fixed + turn * (used - fixed)) % max(1, number_of - fixed)
        return jnp.zeros((number_of,), jnp.int32).at[sequence[jnp.where(places < fixed, places, moved)]].set(jnp.asarray(tallies, jnp.int32))

    tallies = jnp.where(number % 4 == 0, named(heavy_load, number // 4), named(common, number - number // 4 - 1))
    mixed = jax.random.permutation(jax.random.fold_in(own, 3), number_of)
    giver, taker = mixed[0:number_of // 2 * 2:2], mixed[1:number_of // 2 * 2:2]
    room = jnp.minimum(tallies[giver] - 1, limit - tallies[taker]) // 2
    room = jnp.where((giver == sequence[0]) | (taker == sequence[0]) | (tallies[taker] == 0), 0, jnp.maximum(room, 0))
    moved = jax.random.randint(jax.random.fold_in(own, 4), (number_of // 2,), 0, 1 << 20) % (room + 1)
    tallies = tallies.at[giver].add(-moved).at[taker].add(moved)
    members = jnp.searchsorted(jnp.cumsum(tallies), jnp.arange(rows * top), side="right").astype(jnp.int32)
    listing = members.reshape(top, rows).T
    listing = listing[jax.random.permutation(jax.random.fold_in(own, 1), rows)]
    turn = jax.random.randint(jax.random.fold_in(own, 2), (rows, 1), 0, top)
    return jnp.take_along_axis(listing, (jnp.arange(top)[None, :] + turn) % top, axis=1)


def load_shares(count, total, bound, skew, full):
    loads = [(1 << 20) // math.isqrt(grade ** skew) + 1 for grade in range(1, count + 1)]
    largest = bound if full else min(bound, max(-(-total // count), total * loads[0] // sum(loads)))
    least = 1 if total - largest >= count - 1 else 0
    holding, spare = [largest] + [least] * (count - 1), total - largest - least * (count - 1)
    while spare > 0:
        candidates = [i for i in range(1, count) if holding[i] < largest] or [i for i in range(1, count) if holding[i] < bound]
        whole, remaining = sum([loads[i] for i in candidates]), spare
        for i in candidates:
            extra = min(bound - holding[i], max(1, remaining * loads[i] // whole), spare)
            holding[i] = holding[i] + extra
            spare = spare - extra
    return np.array(holding)


def centred(key, shape, width, most, cuts=(), held_as=jnp.bfloat16):
    values = width * jax.random.normal(key, shape, jnp.float32)
    if cuts:
        values = values * block_scale(key, shape, cuts, -0.22, 0.18)
    return jnp.clip(values, -most, most).astype(held_as)


def setup_inputs(seed: int = 0) -> dict:
    streams_of = jax.random.split(jax.random.key(seed), 12)
    volume_field = centred(streams_of[0], (NVEC, NV), 1.0, 6.0, ((1, 128),))
    trace_rows = draw_trace_rows(jax.random.fold_in(streams_of[11], 71), 0)
    near_block = centred(streams_of[2], (NPN, LEAF, LEAF), (LEAF * NEAR_PER) ** -0.5, 0.125, ((0, 128),))
    near_source = touch_ends(jax.random.randint(streams_of[3], (NPN,), 0, TC_DEV), jax.random.fold_in(streams_of[3], 1), 0, TC_DEV - 1).astype(jnp.int32)
    near_offset = touch_ends(jax.random.randint(streams_of[4], (NPN,), 0, 3), jax.random.fold_in(streams_of[4], 1), 0, 2).astype(jnp.int32)
    near_cluster = touch_ends(jax.random.randint(streams_of[5], (NPN,), 0, TC_DEV), jax.random.fold_in(streams_of[5], 1), 0, TC_DEV - 1).astype(jnp.int32)
    far_v = centred(streams_of[6], (NPF, RANK, LEAF), LEAF ** -0.5, 0.5, ((0, 128),))
    far_u = centred(streams_of[7], (NPF, RANK, LEAF), (RANK * FAR_PER) ** -0.5, 0.1875, ((0, 128),))
    far_source = touch_ends(jax.random.randint(streams_of[8], (NPF,), 0, TC_DEV), jax.random.fold_in(streams_of[8], 1), 0, TC_DEV - 1).astype(jnp.int32)
    far_owner_keys = jax.random.split(jax.random.fold_in(streams_of[9], 1), NPF // FP_DEV)
    far_owner_turns = jax.random.permutation(jax.random.fold_in(streams_of[9], 3), NPF // FP_DEV)
    far_owner = jax.vmap(lambda own, number: assign_block(jax.random.fold_in(streams_of[9], 2), own, number, FP_DEV, DEVICES, 1, CAP, 2))(far_owner_keys, far_owner_turns).reshape((NPF, 1))
    far_cluster = touch_ends(jax.random.randint(streams_of[10], (NPF,), 0, TC_DEV), jax.random.fold_in(streams_of[10], 1), 0, TC_DEV - 1).astype(jnp.int32)
    return dict(volume_field=volume_field, trace_rows=trace_rows, near_block=near_block, near_source=near_source, near_offset=near_offset, near_cluster=near_cluster, far_v=far_v, far_u=far_u, far_source=far_source, far_owner=far_owner, far_cluster=far_cluster)


def reference(volume_field, trace_rows, near_block, near_source, near_offset, near_cluster, far_v, far_u, far_source, far_owner, far_cluster):
    columns = jnp.take(volume_field, trace_rows.reshape(-1), axis=1)
    boundary = columns.reshape(NVEC, NCL, LEAF).transpose(1, 0, 2)
    block_near = jnp.arange(NPN, dtype=jnp.int32) // NP_DEV
    near_src = block_near * TC_DEV + near_source
    near_tgt = ((block_near + near_offset - 1) % DEVICES) * TC_DEV + near_cluster
    block_far = jnp.arange(NPF, dtype=jnp.int32) // FP_DEV
    far_src = block_far * TC_DEV + far_source
    far_tgt = far_owner[:, 0] * TC_DEV + far_cluster

    def near_step(total, item):
        blocks, source, target = item
        gathered = boundary[source].astype(jnp.float32)
        terms = jnp.einsum("pij,pvj->pvi", blocks.astype(jnp.float32), gathered)
        return total.at[target].add(terms), None

    def far_step(total, item):
        left, right, source, target = item
        gathered = boundary[source].astype(jnp.float32)
        coeff = jnp.einsum("prl,pvl->prv", left.astype(jnp.float32), gathered).astype(jnp.bfloat16)
        coeff = lax.optimization_barrier(coeff)
        terms = jnp.einsum("prv,prl->pvl", coeff.astype(jnp.float32), right.astype(jnp.float32))
        return total.at[target].add(terms), None

    total = jnp.zeros((NCL, NVEC, LEAF), jnp.float32)
    total, _ = lax.scan(near_step, total, (near_block.reshape(DEVICES, NP_DEV, LEAF, LEAF), near_src.reshape(DEVICES, NP_DEV), near_tgt.reshape(DEVICES, NP_DEV)))
    total, _ = lax.scan(far_step, total, (far_v.reshape(DEVICES, FP_DEV, RANK, LEAF), far_u.reshape(DEVICES, FP_DEV, RANK, LEAF), far_src.reshape(DEVICES, FP_DEV), far_tgt.reshape(DEVICES, FP_DEV)))
    return total
```

```python
import jax
import jax.numpy as jnp
from jax import lax
from jax.experimental import pallas as pl
from jax.experimental.pallas import tpu as pltpu
from jax.sharding import PartitionSpec as P

MESH = pl.DeviceIdType.MESH
F32 = jnp.float32
BF16 = jnp.bfloat16
NT = (((1,), (1,)), ((), ()))

LEAF = 128
NVEC = 16
NDEV = 128
CLUSTERS = 8
SLOTS = 4
NEAR = 128
FAR = 256
RANK = 32
STEPS = 16
PER_STEP = NDEV // STEPS
TILES = 256


def iota(shape, dim):
    return lax.broadcasted_iota(jnp.int32, shape, dim)


def place():
    clu, vol = lax.axis_index("clu"), lax.axis_index("vol")
    return clu // 2, clu % 2, vol // 4, vol % 4


def device(x, core, y, z):
    return (x % 4) * 2 + core % 2, (y % 4) * 4 + z % 4


def partner(k):
    x, core, y, z = place()
    m = (k * 37) % NDEV
    r = m // 2
    clu, vol = device(x + r % 4, core + m % 2, y + (r // 4) % 4, z + r // 16)
    return (clu, vol), clu * 16 + vol


def kernel(
    vol_ref,
    rows_ref,
    nsrc_ref,
    noff_ref,
    nclu_ref,
    fsrc_ref,
    fown_ref,
    fclu_ref,
    near_hbm,
    fv_hbm,
    fu_hbm,
    out_ref,
    table,
    near_vm,
    fv_vm,
    fu_vm,
    bound,
    terms,
    send,
    recv,
    idx_vm,
    idx_sm,
    ids_send,
    ids_recv,
    masks,
    nterm_hi,
    nterm_lo,
    nsum,
    nrecv,
    load_sem,
    idx_sem,
    tab_send,
    tab_recv,
    ids_ssem,
    ids_rsem,
    send_sem,
    recv_sem,
    near_ssem,
    near_rsem,
):
    x, core, y, z = place()
    clu, vol = lax.axis_index("clu"), lax.axis_index("vol")

    loads = [
        pltpu.make_async_copy(fv_hbm, fv_vm, load_sem.at[0]),
        pltpu.make_async_copy(fu_hbm, fu_vm, load_sem.at[1]),
        pltpu.make_async_copy(near_hbm, near_vm, load_sem.at[2]),
    ]
    for load in loads:
        load.start()

    barrier = pltpu.get_barrier_semaphore()

    def greet(k, carry):
        pl.semaphore_signal(barrier, inc=1, device_id=partner(k)[0], device_id_type=MESH)
        return carry

    lax.fori_loop(1, NDEV, greet, 0)

    base = vol * 16
    for hi in range(16):
        table[base + hi] = vol_ref[:, hi * LEAF : (hi + 1) * LEAF]

    owns = iota((NDEV, FAR), 0) == fown_ref[...]
    upto = (iota((FAR, FAR), 0) <= iota((FAR, FAR), 1)).astype(F32).astype(BF16)
    count = jnp.dot(owns.astype(F32).astype(BF16), upto, preferred_element_type=F32)
    number = (iota((16, FAR), 1) + 1).astype(F32).astype(BF16)
    clusters = fclu_ref[...].astype(F32)
    slot_of_lane = (iota((NDEV, LEAF), 1) // NVEC) % SLOTS
    ids = jnp.zeros((NDEV, LEAF), F32)
    for j in range(SLOTS):
        chosen = jnp.where(owns & (count == float(j + 1)), 1.0, 0.0)
        found = lax.dot_general(number, chosen.astype(BF16), NT, preferred_element_type=F32)
        idx_vm[j : j + 1, :] = found[0:1, :].astype(jnp.int32)
        target = jnp.sum(chosen * clusters, axis=1, keepdims=True)
        ids = jnp.where(slot_of_lane == j, target, ids)
    ids_send[...] = ids.reshape(NDEV, 1, LEAF)
    to_smem = pltpu.make_async_copy(idx_vm, idx_sm, idx_sem)
    to_smem.start()

    pl.semaphore_wait(barrier, NDEV - 1)

    def half(dy, dz, h):
        owner = ((y - dy + 4) % 4) * 4 + (z - dz + 4) % 4
        return table.at[pl.ds(owner * 16 + h * 8, 8)]

    def pass_on(dy, dz, h, ey, ez):
        block = half(dy, dz, h)
        pltpu.make_async_remote_copy(
            src_ref=block,
            dst_ref=block,
            send_sem=tab_send,
            recv_sem=tab_recv.at[h * 16 + (dy + ey) * 4 + dz + ez],
            device_id=(clu, ((y + ey) % 4) * 4 + (z + ez) % 4),
            device_id_type=MESH,
        ).start()

    def arrived(dy, dz, h):
        block = half(dy, dz, h)
        pltpu.make_async_copy(block, block, tab_recv.at[h * 16 + dy * 4 + dz]).wait()

    order = (1, 3, 2)
    for e in order:
        pass_on(0, 0, 0, 0, e)
        pass_on(0, 0, 1, e, 0)
    for e in order:
        pass_on(0, 0, 0, e, 0)
        pass_on(0, 0, 1, 0, e)

    def send_ids(k, carry):
        dev, flat = partner(k)
        pltpu.make_async_remote_copy(
            src_ref=ids_send.at[flat],
            dst_ref=ids_recv.at[k],
            send_sem=ids_ssem,
            recv_sem=ids_rsem,
            device_id=dev,
            device_id_type=MESH,
        ).start()
        return carry

    for d in order:
        arrived(0, d, 0)
        for e in order:
            pass_on(0, d, 0, e, 0)
        arrived(d, 0, 1)
        for e in order:
            pass_on(d, 0, 1, 0, e)
    lax.fori_loop(1, NDEV, send_ids, 0)
    ids_recv[0] = ids_send[clu * 16 + vol]

    for d in order:
        arrived(d, 0, 0)
        arrived(0, d, 1)
    for d in order:
        for e in order:
            arrived(d, e, 0)
            arrived(d, e, 1)

    lane = iota((NVEC, LEAF), 1)

    def gather(c, carry):
        got = jnp.zeros((NVEC, LEAF), F32)
        for n in range(LEAF):
            row = rows_ref[c, n] & (TILES * LEAF - 1)
            tile = table[lax.shift_right_logical(row, 7)].astype(F32)
            got = jnp.where(lane == n, pltpu.roll(tile, (n - row) & (LEAF - 1), axis=1), got)
        bound[c] = got.astype(BF16)
        return carry

    lax.fori_loop(0, CLUSTERS, gather, 0)

    loads[0].wait()
    loads[1].wait()
    same = iota((8 * NVEC, 8 * RANK), 0) // NVEC == iota((8 * NVEC, 8 * RANK), 1) // RANK
    terms[0] = jnp.zeros((NVEC, LEAF), BF16)

    def far(g, carry):
        first = g * 8
        lhs = jnp.concatenate([bound[fsrc_ref[first + i]] for i in range(8)], axis=0)
        v = fv_vm[pl.ds(first, 8)].reshape(8 * RANK, LEAF)
        u = fu_vm[pl.ds(first, 8)].reshape(8 * RANK, LEAF)
        coeff = lax.dot_general(lhs, v, NT, preferred_element_type=F32)
        coeff = jnp.where(same, coeff, 0.0).astype(BF16)
        term = jnp.dot(coeff, u, preferred_element_type=F32)
        terms[pl.ds(first + 1, 8)] = term.astype(BF16).reshape(8, NVEC, LEAF)
        return carry

    lax.fori_loop(0, FAR // 8, far, 0)

    to_smem.wait()
    me = clu * 16 + vol
    for j in range(SLOTS):
        recv[0, j * NVEC : (j + 1) * NVEC, :] = terms[jnp.clip(idx_sm[j, me], 0, FAR)]

    def send_terms(k, carry):
        dev, flat = partner(k)
        for j in range(SLOTS):
            send[k, j * NVEC : (j + 1) * NVEC, :] = terms[jnp.clip(idx_sm[j, flat], 0, FAR)]
        pltpu.make_async_remote_copy(
            src_ref=send.at[k],
            dst_ref=recv.at[k],
            send_sem=send_sem,
            recv_sem=recv_sem.at[k // PER_STEP],
            device_id=dev,
            device_id_type=MESH,
        ).start()
        return carry

    lax.fori_loop(1, NDEV, send_terms, 0)

    loads[2].wait()

    def near(g, carry):
        first = g * 8
        for i in range(8):
            term = lax.dot_general(bound[nsrc_ref[first + i]], near_vm[first + i], NT, preferred_element_type=F32)
            high = term.astype(BF16)
            nterm_hi[first + i] = high
            nterm_lo[first + i] = (term - high.astype(F32)).astype(BF16)
        return carry

    lax.fori_loop(0, NEAR // 8, near, 0)

    rows = 3 * CLUSTERS * NVEC
    named = (noff_ref[...] * CLUSTERS + nclu_ref[...]).astype(F32).astype(BF16)
    named = jnp.broadcast_to(named, (16, NEAR))
    vec_row = iota((rows, 256), 0) % NVEC == iota((rows, 256), 1) % NVEC
    target_row = (iota((rows, 256), 0) // NVEC).astype(F32)
    nsum[...] = jnp.zeros_like(nsum)

    def near_sum(g, carry):
        first = g * 16
        spread = (iota((NEAR, 256), 0) == first + iota((NEAR, 256), 1) // NVEC).astype(F32).astype(BF16)
        wanted = jnp.dot(named, spread, preferred_element_type=F32)[0:1, :]
        pick = jnp.where(vec_row & (target_row == wanted), 1.0, 0.0).astype(BF16)
        high = nterm_hi[pl.ds(first, 16)].reshape(256, LEAF)
        low = nterm_lo[pl.ds(first, 16)].reshape(256, LEAF)
        total = jnp.dot(pick, high, preferred_element_type=F32) + jnp.dot(pick, low, preferred_element_type=F32)
        nsum[...] += total.reshape(3 * CLUSTERS, NVEC, LEAF)
        return carry

    lax.fori_loop(0, NEAR // 16, near_sum, 0)

    before, after = (me + NDEV - 1) % NDEV, (me + 1) % NDEV
    near_copies = []
    for i, (block, to) in enumerate(((0, before), (2, after))):
        copy = pltpu.make_async_remote_copy(
            src_ref=nsum.at[pl.ds(block * CLUSTERS, CLUSTERS)],
            dst_ref=nrecv.at[i],
            send_sem=near_ssem.at[i],
            recv_sem=near_rsem.at[i],
            device_id=(to // 16, to % 16),
            device_id_type=MESH,
        )
        copy.start()
        near_copies.append(copy)

    pltpu.make_async_copy(ids_recv.at[pl.ds(1, NDEV - 1)], ids_recv.at[pl.ds(1, NDEV - 1)], ids_rsem).wait()
    vec_same = iota((LEAF, LEAF), 0) % NVEC == iota((LEAF, LEAF), 1) % NVEC
    cluster_row = (iota((LEAF, LEAF), 0) // NVEC).astype(F32)
    left = iota((1, LEAF), 1) < LEAF // 2

    def make_mask(g, carry):
        wanted = jnp.where(left, ids_recv[g * 2], ids_recv[g * 2 + 1])
        masks[g] = jnp.where(vec_same & (cluster_row == wanted), 1.0, 0.0).astype(BF16)
        return carry

    lax.fori_loop(0, NDEV // 2, make_mask, 0)

    total = nsum[pl.ds(CLUSTERS, CLUSTERS)].reshape(CLUSTERS * NVEC, LEAF)
    for s in range(STEPS):
        lo = max(1, s * PER_STEP)
        part = recv.at[pl.ds(lo, (s + 1) * PER_STEP - lo)]
        pltpu.make_async_copy(part, part, recv_sem.at[s]).wait()
        for t in range(PER_STEP // 4):
            g = s * PER_STEP // 2 + t * 2
            pick = jnp.concatenate([masks[g], masks[g + 1]], axis=1)
            block = recv[pl.ds(g * 2, 4)].reshape(4 * SLOTS * NVEC, LEAF)
            total += jnp.dot(pick, block, preferred_element_type=F32)
    for copy in near_copies:
        copy.wait()
    total = total.reshape(CLUSTERS, NVEC, LEAF)
    out_ref[...] = total + nrecv[0] + nrecv[1]

    sent = table.at[pl.ds(0, 240)]
    pltpu.make_async_copy(sent, sent, tab_send).wait()
    sent = ids_send.at[pl.ds(1, NDEV - 1)]
    pltpu.make_async_copy(sent, sent, ids_ssem).wait()
    sent = send.at[pl.ds(1, NDEV - 1)]
    pltpu.make_async_copy(sent, sent, send_sem).wait()


def body(
    volume_field,
    trace_rows,
    near_block,
    near_source,
    near_offset,
    near_cluster,
    far_v,
    far_u,
    far_source,
    far_owner,
    far_cluster,
):
    vmem = pl.BlockSpec(memory_space=pltpu.VMEM)
    smem = pl.BlockSpec(memory_space=pltpu.SMEM)
    hbm = pl.BlockSpec(memory_space=pl.ANY)
    dma = pltpu.SemaphoreType.DMA
    return pl.pallas_call(
        kernel,
        out_shape=jax.ShapeDtypeStruct((CLUSTERS, NVEC, LEAF), F32),
        in_specs=[vmem, smem, smem, vmem, vmem, smem, vmem, vmem, hbm, hbm, hbm],
        out_specs=vmem,
        scratch_shapes=[
            pltpu.VMEM((TILES, NVEC, LEAF), BF16),
            pltpu.VMEM((NEAR, LEAF, LEAF), BF16),
            pltpu.VMEM((FAR, RANK, LEAF), BF16),
            pltpu.VMEM((FAR, RANK, LEAF), BF16),
            pltpu.VMEM((CLUSTERS, NVEC, LEAF), BF16),
            pltpu.VMEM((FAR + 8, NVEC, LEAF), BF16),
            pltpu.VMEM((NDEV, SLOTS * NVEC, LEAF), BF16),
            pltpu.VMEM((NDEV, SLOTS * NVEC, LEAF), BF16),
            pltpu.VMEM((8, NDEV), jnp.int32),
            pltpu.SMEM((8, NDEV), jnp.int32),
            pltpu.VMEM((NDEV, 1, LEAF), F32),
            pltpu.VMEM((NDEV, 1, LEAF), F32),
            pltpu.VMEM((NDEV // 2, LEAF, LEAF), BF16),
            pltpu.VMEM((NEAR, NVEC, LEAF), BF16),
            pltpu.VMEM((NEAR, NVEC, LEAF), BF16),
            pltpu.VMEM((3 * CLUSTERS, NVEC, LEAF), F32),
            pltpu.VMEM((2, CLUSTERS, NVEC, LEAF), F32),
            dma((3,)),
            dma,
            dma,
            dma((32,)),
            dma,
            dma,
            dma,
            dma((STEPS,)),
            dma((2,)),
            dma((2,)),
        ],
        compiler_params=pltpu.CompilerParams(
            collective_id=0, has_side_effects=True, vmem_limit_bytes=40 * 2**20
        ),
        cost_estimate=pl.CostEstimate(flops=2 * 10**8, bytes_accessed=9 * 2**20, transcendentals=0),
    )(
        volume_field,
        trace_rows,
        near_source,
        near_offset.reshape(1, NEAR),
        near_cluster.reshape(1, NEAR),
        far_source,
        far_owner.reshape(1, FAR),
        far_cluster.reshape(1, FAR),
        near_block,
        far_v,
        far_u,
    )


def solution(mesh):
    both = ("clu", "vol")
    return jax.shard_map(
        body,
        mesh=mesh,
        in_specs=(
            P(None, both),
            P(both, None),
            P(both, None, None),
            P(both),
            P(both),
            P(both),
            P(both, None, None),
            P(both, None, None),
            P(both),
            P(both, None),
            P(both),
        ),
        out_specs=P(both, None, None),
        check_vma=False,
    )
```

```python
import jax
import jax.numpy as jnp
from jax import lax
from jax.experimental import pallas as pl
from jax.experimental.pallas import tpu as pltpu
from jax.sharding import PartitionSpec as P

MESH = pl.DeviceIdType.MESH
F32 = jnp.float32
BF16 = jnp.bfloat16
NT = (((1,), (1,)), ((), ()))

LEAF = 128
NVEC = 16
NDEV = 128
CLUSTERS = 8
SLOTS = 4
NEAR = 128
FAR = 256
RANK = 32
STEPS = 16
PER_STEP = NDEV // STEPS
TILES = 256


def iota(shape, dim):
    return lax.broadcasted_iota(jnp.int32, shape, dim)


def place():
    clu, vol = lax.axis_index("clu"), lax.axis_index("vol")
    return lax.div(clu, 2), lax.rem(clu, 2), lax.div(vol, 4), lax.rem(vol, 4)


def partner(k, sign):
    x, core, y, z = place()
    m = lax.rem(k * 37, NDEV)
    r = lax.div(m, 2)
    dx, dy, dz = lax.rem(r, 4), lax.rem(lax.div(r, 4), 4), lax.div(r, 16)
    clu = lax.rem(x + 4 + sign * dx, 4) * 2 + lax.rem(core + m, 2)
    vol = lax.rem(y + 4 + sign * dy, 4) * 4 + lax.rem(z + 4 + sign * dz, 4)
    return clu, vol


def kernel(
    vol_hbm,
    rows_hbm,
    nsrc_hbm,
    noff_hbm,
    nclu_hbm,
    fsrc_hbm,
    fown_hbm,
    fclu_hbm,
    near_hbm,
    fv_hbm,
    fu_hbm,
    out_ref,
    vol_ref,
    rows_ref,
    nsrc_ref,
    noff_ref,
    nclu_ref,
    fsrc_ref,
    fown_ref,
    fclu_ref,
    table,
    near_vm,
    fv_vm,
    fu_vm,
    bound,
    send,
    recv,
    idx_vm,
    idx_sm,
    ids_send,
    ids_half,
    ids_recv,
    masks,
    nterm_hi,
    nterm_lo,
    nsum,
    nrecv,
    load_sem,
    idx_sem,
    tab_send,
    tab_recv,
    ids_ssem,
    ids_rsem,
    sync,
    send_sem,
    recv_sem,
    near_ssem,
    near_rsem,
):
    x, core, y, z = place()
    clu, vol = lax.axis_index("clu"), lax.axis_index("vol")

    barrier = pltpu.get_barrier_semaphore()

    def along_clu(k):
        return lax.rem(clu + k, 8), vol

    def along(ey, ez):
        return clu, lax.rem(y + ey, 4) * 4 + lax.rem(z + ez, 4)

    near_by = [along_clu(k) for k in range(1, 8)]
    near_by += [along(e, 0) for e in range(1, 4)] + [along(0, e) for e in range(1, 4)]
    for dev in near_by:
        pl.semaphore_signal(barrier, inc=1, device_id=dev, device_id_type=MESH)

    pairs = (
        (vol_hbm, vol_ref),
        (fown_hbm, fown_ref),
        (fclu_hbm, fclu_ref),
        (rows_hbm, rows_ref),
        (fsrc_hbm, fsrc_ref),
        (fv_hbm, fv_vm),
        (fu_hbm, fu_vm),
        (nsrc_hbm, nsrc_ref),
        (noff_hbm, noff_ref),
        (nclu_hbm, nclu_ref),
        (near_hbm, near_vm),
    )
    loads = [pltpu.make_async_copy(a, b, load_sem.at[i]) for i, (a, b) in enumerate(pairs)]
    for load in loads:
        load.start()
    for load in loads[:3]:
        load.wait()

    base = vol * 16
    for hi in range(16):
        table[base + hi] = vol_ref[:, hi * LEAF : (hi + 1) * LEAF]

    owns = iota((NDEV, FAR), 0) == fown_ref[...]
    upto = (iota((FAR, FAR), 0) <= iota((FAR, FAR), 1)).astype(F32).astype(BF16)
    count = jnp.dot(owns.astype(F32).astype(BF16), upto, preferred_element_type=F32)
    number = iota((16, FAR), 1).astype(F32).astype(BF16)
    clusters = fclu_ref[...].astype(F32) + 1.0
    slot_of_lane = (iota((NDEV, LEAF), 1) // NVEC) % SLOTS
    ids = jnp.zeros((NDEV, LEAF), F32)
    for j in range(SLOTS):
        chosen = jnp.where(owns & (count == float(j + 1)), 1.0, 0.0)
        found = lax.dot_general(number, chosen.astype(BF16), NT, preferred_element_type=F32)
        idx_vm[j : j + 1, :] = found[0:1, :].astype(jnp.int32)
        target = jnp.sum(chosen * clusters, axis=1, keepdims=True) - 1.0
        ids = jnp.where(slot_of_lane == j, target, ids)
    ids_send[...] = ids.reshape(NDEV, 1, LEAF)
    to_smem = pltpu.make_async_copy(idx_vm, idx_sm, idx_sem)
    to_smem.start()

    pl.semaphore_wait(barrier, len(near_by))

    def half(dy, dz, h):
        owner = lax.rem(y + 4 - dy, 4) * 4 + lax.rem(z + 4 - dz, 4)
        return table.at[pl.ds(owner * 16 + h * 8, 8)]

    def pass_on(dy, dz, h, ey, ez):
        block = half(dy, dz, h)
        pltpu.make_async_remote_copy(
            src_ref=block,
            dst_ref=block,
            send_sem=tab_send,
            recv_sem=tab_recv.at[h * 16 + (dy + ey) * 4 + dz + ez],
            device_id=along(ey, ez),
            device_id_type=MESH,
        ).start()

    def arrived(dy, dz, h):
        block = half(dy, dz, h)
        pltpu.make_async_copy(block, block, tab_recv.at[h * 16 + dy * 4 + dz]).wait()

    order = (1, 3, 2)
    for e in order:
        pass_on(0, 0, 0, 0, e)
        pass_on(0, 0, 1, e, 0)
    for e in order:
        pass_on(0, 0, 0, e, 0)
        pass_on(0, 0, 1, 0, e)

    for k in range(1, 8):
        dev = along_clu(k)
        pltpu.make_async_remote_copy(
            src_ref=ids_send.at[pl.ds(dev[0] * 16, 16)],
            dst_ref=ids_half.at[clu],
            send_sem=ids_ssem.at[0],
            recv_sem=ids_rsem.at[0],
            device_id=dev,
            device_id_type=MESH,
        ).start()
    ids_half[clu] = ids_send[pl.ds(clu * 16, 16)]

    for d in order:
        arrived(0, d, 0)
        for e in order:
            pass_on(0, d, 0, e, 0)
        arrived(d, 0, 1)
        for e in order:
            pass_on(d, 0, 1, 0, e)
    for d in order:
        arrived(d, 0, 0)
        arrived(0, d, 1)
    for d in order:
        for e in order:
            arrived(d, e, 0)
            arrived(d, e, 1)

    for k in range(1, 8):
        pl.semaphore_signal(sync, inc=1, device_id=along_clu(k), device_id_type=MESH)

    part = ids_half.at[pl.ds(0, 7)]
    pltpu.make_async_copy(part, part, ids_rsem.at[0]).wait()
    for k in range(1, 16):
        there = lax.rem(vol + k, 16)
        pltpu.make_async_remote_copy(
            src_ref=ids_half.at[:, there],
            dst_ref=ids_recv.at[vol],
            send_sem=ids_ssem.at[1],
            recv_sem=ids_rsem.at[1],
            device_id=(clu, there),
            device_id_type=MESH,
        ).start()
    ids_recv[vol] = ids_half[:, vol]

    loads[3].wait()
    lane = iota((NVEC, LEAF), 1)

    def gather(c, carry):
        got = jnp.zeros((NVEC, LEAF), F32)
        for n in range(LEAF):
            row = rows_ref[c, n] & (TILES * LEAF - 1)
            tile = table[lax.shift_right_logical(row, 7)].astype(F32)
            got = jnp.where(lane == n, pltpu.roll(tile, (n - row) & (LEAF - 1), axis=1), got)
        bound[c] = got.astype(BF16)
        return carry

    lax.fori_loop(0, CLUSTERS, gather, 0)

    for load in loads[4:7]:
        load.wait()
    to_smem.wait()
    same = iota((8 * NVEC, 8 * RANK), 0) // NVEC == iota((8 * NVEC, 8 * RANK), 1) // RANK
    me = clu * 16 + vol

    def far(i):
        devs = [partner(i * 2 + a, 1) for a in range(2)]
        pairs = [
            jnp.clip(idx_sm[j, dev[0] * 16 + dev[1]], 0, FAR - 1) for dev in devs for j in range(SLOTS)
        ]
        lhs = jnp.concatenate([bound[fsrc_ref[q]] for q in pairs], axis=0)
        v = jnp.concatenate([fv_vm[q] for q in pairs], axis=0)
        u = jnp.concatenate([fu_vm[q] for q in pairs], axis=0)
        coeff = lax.dot_general(lhs, v, NT, preferred_element_type=F32)
        coeff = jnp.where(same, coeff, 0.0).astype(BF16)
        term = jnp.dot(coeff, u, preferred_element_type=F32).astype(BF16)
        return devs, term.reshape(2, SLOTS * NVEC, LEAF)

    def send_term(k, dev):
        pltpu.make_async_remote_copy(
            src_ref=send.at[k],
            dst_ref=recv.at[k],
            send_sem=send_sem,
            recv_sem=recv_sem.at[lax.div(k, PER_STEP)],
            device_id=dev,
            device_id_type=MESH,
        ).start()

    devs, term = far(0)
    recv[0] = term[0]
    send[1] = term[1]
    pl.semaphore_wait(sync, 7)
    send_term(1, devs[1])

    def far_step(i, carry):
        devs, term = far(i)
        send[pl.ds(i * 2, 2)] = term
        for a in range(2):
            send_term(i * 2 + a, devs[a])
        return carry

    lax.fori_loop(1, NDEV // 2, far_step, 0, unroll=3)

    for load in loads[7:]:
        load.wait()

    def near(g, carry):
        first = g * 8
        for i in range(8):
            term = lax.dot_general(bound[nsrc_ref[first + i]], near_vm[first + i], NT, preferred_element_type=F32)
            high = term.astype(BF16)
            nterm_hi[first + i] = high
            nterm_lo[first + i] = (term - high.astype(F32)).astype(BF16)
        return carry

    lax.fori_loop(0, NEAR // 8, near, 0)

    rows = 3 * CLUSTERS * NVEC
    named = (noff_ref[...] * CLUSTERS + nclu_ref[...]).astype(F32).astype(BF16)
    named = jnp.broadcast_to(named, (16, NEAR))
    vec_row = iota((rows, 256), 0) % NVEC == iota((rows, 256), 1) % NVEC
    target_row = (iota((rows, 256), 0) // NVEC).astype(F32)
    nsum[...] = jnp.zeros_like(nsum)

    def near_sum(g, carry):
        first = g * 16
        spread = (iota((NEAR, 256), 0) == first + iota((NEAR, 256), 1) // NVEC).astype(F32).astype(BF16)
        wanted = jnp.dot(named, spread, preferred_element_type=F32)[0:1, :]
        pick = jnp.where(vec_row & (target_row == wanted), 1.0, 0.0).astype(BF16)
        high = nterm_hi[pl.ds(first, 16)].reshape(256, LEAF)
        low = nterm_lo[pl.ds(first, 16)].reshape(256, LEAF)
        total = jnp.dot(pick, high, preferred_element_type=F32) + jnp.dot(pick, low, preferred_element_type=F32)
        nsum[...] += total.reshape(3 * CLUSTERS, NVEC, LEAF)
        return carry

    lax.fori_loop(0, NEAR // 16, near_sum, 0)

    before, after = lax.rem(me + NDEV - 1, NDEV), lax.rem(me + 1, NDEV)
    near_copies = []
    for i, (block, to) in enumerate(((0, before), (2, after))):
        copy = pltpu.make_async_remote_copy(
            src_ref=nsum.at[pl.ds(block * CLUSTERS, CLUSTERS)],
            dst_ref=nrecv.at[i],
            send_sem=near_ssem.at[i],
            recv_sem=near_rsem.at[i],
            device_id=(lax.div(to, 16), lax.rem(to, 16)),
            device_id_type=MESH,
        )
        copy.start()
        near_copies.append(copy)

    part = ids_recv.at[pl.ds(0, 15)]
    pltpu.make_async_copy(part, part, ids_rsem.at[1]).wait()
    vec_same = iota((LEAF, LEAF), 0) % NVEC == iota((LEAF, LEAF), 1) % NVEC
    cluster_row = (iota((LEAF, LEAF), 0) // NVEC).astype(F32)
    left = iota((1, LEAF), 1) < LEAF // 2

    def make_mask(g, carry):
        origins = [partner(g * 2 + a, -1) for a in range(2)]
        one, two = [ids_recv[origin[1], origin[0]] for origin in origins]
        wanted = jnp.where(left, one, two)
        masks[g] = jnp.where(vec_same & (cluster_row == wanted), 1.0, 0.0).astype(BF16)
        return carry

    lax.fori_loop(0, NDEV // 2, make_mask, 0)

    total = nsum[pl.ds(CLUSTERS, CLUSTERS)].reshape(CLUSTERS * NVEC, LEAF)
    for s in range(STEPS):
        lo = max(1, s * PER_STEP)
        part = recv.at[pl.ds(lo, (s + 1) * PER_STEP - lo)]
        pltpu.make_async_copy(part, part, recv_sem.at[s]).wait()
        for t in range(PER_STEP // 4):
            g = s * PER_STEP // 2 + t * 2
            pick = jnp.concatenate([masks[g], masks[g + 1]], axis=1)
            block = recv[pl.ds(g * 2, 4)].reshape(4 * SLOTS * NVEC, LEAF)
            total += jnp.dot(pick, block, preferred_element_type=F32)
    for copy in near_copies:
        copy.wait()
    total = total.reshape(CLUSTERS, NVEC, LEAF)
    out_ref[...] = total + nrecv[0] + nrecv[1]

    sent = table.at[pl.ds(0, 240)]
    pltpu.make_async_copy(sent, sent, tab_send).wait()
    sent = ids_half.at[pl.ds(0, 7)]
    pltpu.make_async_copy(sent, sent, ids_ssem.at[0]).wait()
    sent = ids_recv.at[pl.ds(0, 15)]
    pltpu.make_async_copy(sent, sent, ids_ssem.at[1]).wait()
    sent = send.at[pl.ds(1, NDEV - 1)]
    pltpu.make_async_copy(sent, sent, send_sem).wait()


def body(
    volume_field,
    trace_rows,
    near_block,
    near_source,
    near_offset,
    near_cluster,
    far_v,
    far_u,
    far_source,
    far_owner,
    far_cluster,
):
    vmem = pl.BlockSpec(memory_space=pltpu.VMEM)
    hbm = pl.BlockSpec(memory_space=pltpu.HBM)
    dma = pltpu.SemaphoreType.DMA
    return pl.pallas_call(
        kernel,
        out_shape=jax.ShapeDtypeStruct((CLUSTERS, NVEC, LEAF), F32),
        in_specs=[hbm] * 11,
        out_specs=vmem,
        scratch_shapes=[
            pltpu.VMEM((NVEC, TILES // 16 * LEAF), BF16),
            pltpu.SMEM((CLUSTERS, LEAF), jnp.int32),
            pltpu.SMEM((NEAR,), jnp.int32),
            pltpu.VMEM((1, NEAR), jnp.int32),
            pltpu.VMEM((1, NEAR), jnp.int32),
            pltpu.SMEM((FAR,), jnp.int32),
            pltpu.VMEM((1, FAR), jnp.int32),
            pltpu.VMEM((1, FAR), jnp.int32),
            pltpu.VMEM((TILES, NVEC, LEAF), BF16),
            pltpu.VMEM((NEAR, LEAF, LEAF), BF16),
            pltpu.VMEM((FAR, RANK, LEAF), BF16),
            pltpu.VMEM((FAR, RANK, LEAF), BF16),
            pltpu.VMEM((CLUSTERS, NVEC, LEAF), BF16),
            pltpu.VMEM((NDEV, SLOTS * NVEC, LEAF), BF16),
            pltpu.VMEM((NDEV, SLOTS * NVEC, LEAF), BF16),
            pltpu.VMEM((8, NDEV), jnp.int32),
            pltpu.SMEM((8, NDEV), jnp.int32),
            pltpu.VMEM((NDEV, 1, LEAF), F32),
            pltpu.VMEM((8, 16, 1, LEAF), F32),
            pltpu.VMEM((16, 8, 1, LEAF), F32),
            pltpu.VMEM((NDEV // 2, LEAF, LEAF), BF16),
            pltpu.VMEM((NEAR, NVEC, LEAF), BF16),
            pltpu.VMEM((NEAR, NVEC, LEAF), BF16),
            pltpu.VMEM((3 * CLUSTERS, NVEC, LEAF), F32),
            pltpu.VMEM((2, CLUSTERS, NVEC, LEAF), F32),
            dma((11,)),
            dma,
            dma,
            dma((32,)),
            dma((2,)),
            dma((2,)),
            pltpu.SemaphoreType.REGULAR,
            dma,
            dma((STEPS,)),
            dma((2,)),
            dma((2,)),
        ],
        compiler_params=pltpu.CompilerParams(
            collective_id=0, has_side_effects=True, vmem_limit_bytes=40 * 2**20
        ),
        cost_estimate=pl.CostEstimate(flops=2 * 10**8, bytes_accessed=9 * 2**20, transcendentals=0),
    )(
        *(pltpu.with_memory_space_constraint(a, pltpu.HBM) for a in (
        volume_field,
        trace_rows,
        near_source,
        near_offset.reshape(1, NEAR),
        near_cluster.reshape(1, NEAR),
        far_source,
        far_owner.reshape(1, FAR),
        far_cluster.reshape(1, FAR),
        near_block,
        far_v,
        far_u,
    )))


def solution(mesh):
    both = ("clu", "vol")
    return jax.shard_map(
        body,
        mesh=mesh,
        in_specs=(
            P(None, both),
            P(both, None),
            P(both, None, None),
            P(both),
            P(both),
            P(both),
            P(both, None, None),
            P(both, None, None),
            P(both),
            P(both, None),
            P(both),
        ),
        out_specs=P(both, None, None),
        check_vma=False,
    )
```

```python
import jax
import jax.numpy as jnp
from jax import lax
from jax.experimental import pallas as pl
from jax.experimental.pallas import tpu as pltpu
from jax.sharding import PartitionSpec as P

MESH = pl.DeviceIdType.MESH
F32 = jnp.float32
BF16 = jnp.bfloat16
NT = (((1,), (1,)), ((), ()))

LEAF = 128
NVEC = 16
NDEV = 128
CLUSTERS = 8
SLOTS = 4
NEAR = 128
FAR = 256
RANK = 32
STEPS = 16
SPLIT = 4
HALF = 8
TILES = 256


def iota(shape, dim):
    return lax.broadcasted_iota(jnp.int32, shape, dim)


def place():
    clu, vol = lax.axis_index("clu"), lax.axis_index("vol")
    return lax.div(clu, 2), lax.rem(clu, 2), lax.div(vol, 4), lax.rem(vol, 4)


def at(dx, dcore, dy, dz):
    x, core, y, z = place()
    clu = lax.rem(x + dx, 4) * 2 + lax.rem(core + dcore, 2)
    return clu, lax.rem(y + dy, 4) * 4 + lax.rem(z + dz, 4)


def member(s, g):
    return at(lax.div(g, 2), lax.rem(g, 2), 0, 0) if s < HALF else at(0, lax.rem(g, 2), lax.div(g, 2), 0)


def offset(along_y, p):
    if along_y:
        return lax.rem(lax.div(p, 2) + 1, 4), 1 + 2 * lax.rem(p, 2)
    return lax.rem(p + 1, 4), 2 - 2 * lax.div(p, 4)


def owner(along_y, g, p):
    d, dz = offset(along_y, p)
    return at(d, lax.rem(g, 2), lax.div(g, 2), dz) if along_y else at(lax.div(g, 2), lax.rem(g, 2), d, dz)


def kernel(
    vol_hbm,
    rows_hbm,
    nsrc_hbm,
    noff_hbm,
    nclu_hbm,
    fsrc_hbm,
    fown_hbm,
    fclu_hbm,
    near_hbm,
    fv_hbm,
    fu_hbm,
    out_ref,
    vol_ref,
    rows_ref,
    nsrc_ref,
    noff_ref,
    nclu_ref,
    fsrc_ref,
    fown_ref,
    fclu_ref,
    table,
    near_vm,
    fv_vm,
    fu_vm,
    bound,
    send,
    recv,
    wide_send,
    wide_recv,
    idx_vm,
    idx_sm,
    ids_all,
    ids_send,
    ids_recv,
    masks,
    nterm_hi,
    nterm_lo,
    nsum,
    nrecv,
    load_sem,
    idx_sem,
    tab_send,
    tab_recv,
    ids_ssem,
    ids_rsem,
    send_sem,
    recv_sem,
    wide_ssem,
    wide_rsem,
    near_ssem,
    near_rsem,
):
    x, core, y, z = place()
    clu, vol = lax.axis_index("clu"), lax.axis_index("vol")

    barrier = pltpu.get_barrier_semaphore()

    def along_clu(k):
        return lax.rem(clu + k, 8), vol

    def along(ey, ez):
        return clu, lax.rem(y + ey, 4) * 4 + lax.rem(z + ez, 4)

    near_by = [along_clu(k) for k in range(1, 8)]
    near_by += [at(0, c, e, 0) for c in range(2) for e in range(1, 4)] + [along(0, e) for e in range(1, 4)]
    for dev in near_by:
        pl.semaphore_signal(barrier, inc=1, device_id=dev, device_id_type=MESH)

    pairs = (
        (vol_hbm, vol_ref),
        (fown_hbm, fown_ref),
        (fclu_hbm, fclu_ref),
        (rows_hbm, rows_ref),
        (fsrc_hbm, fsrc_ref),
        (fv_hbm, fv_vm),
        (fu_hbm, fu_vm),
        (nsrc_hbm, nsrc_ref),
        (noff_hbm, noff_ref),
        (nclu_hbm, nclu_ref),
        (near_hbm, near_vm),
    )
    loads = [pltpu.make_async_copy(a, b, load_sem.at[i]) for i, (a, b) in enumerate(pairs)]
    for load in loads:
        load.start()
    for load in loads[:3]:
        load.wait()

    base = vol * 16
    for hi in range(16):
        table[base + hi] = vol_ref[:, hi * LEAF : (hi + 1) * LEAF]

    owns = iota((NDEV, FAR), 0) == fown_ref[...]
    upto = (iota((FAR, FAR), 0) <= iota((FAR, FAR), 1)).astype(F32).astype(BF16)
    count = jnp.dot(owns.astype(F32).astype(BF16), upto, preferred_element_type=F32)
    number = iota((16, FAR), 1).astype(F32).astype(BF16)
    clusters = fclu_ref[...].astype(F32) + 1.0
    slot_of_lane = (iota((NDEV, LEAF), 1) // NVEC) % SLOTS
    ids = jnp.zeros((NDEV, LEAF), F32)
    for j in range(SLOTS):
        chosen = jnp.where(owns & (count == float(j + 1)), 1.0, 0.0)
        found = lax.dot_general(number, chosen.astype(BF16), NT, preferred_element_type=F32)
        idx_vm[j : j + 1, :] = found[0:1, :].astype(jnp.int32)
        target = jnp.sum(chosen * clusters, axis=1, keepdims=True) - 1.0
        ids = jnp.where(slot_of_lane == j, target, ids)
    ids_all[...] = ids.reshape(NDEV, 1, LEAF)
    for s in (0, HALF):
        for g in range(8):

            def ids_row(p, carry, s=s, g=g):
                dev = owner(s >= HALF, g, p)
                ids_send[s + g, p] = ids_all[dev[0] * 16 + dev[1]]
                return carry

            lax.fori_loop(0, HALF, ids_row, 0, unroll=4)
    to_smem = pltpu.make_async_copy(idx_vm, idx_sm, idx_sem)
    to_smem.start()

    pl.semaphore_wait(barrier, len(near_by))

    def half(dy, dz, h):
        owner = lax.rem(y + 4 - dy, 4) * 4 + lax.rem(z + 4 - dz, 4)
        return table.at[pl.ds(owner * 16 + h * 8, 8)]

    def pass_on(dy, dz, h, ey, ez):
        block = half(dy, dz, h)
        pltpu.make_async_remote_copy(
            src_ref=block,
            dst_ref=block,
            send_sem=tab_send,
            recv_sem=tab_recv.at[h * 16 + (dy + ey) * 4 + dz + ez],
            device_id=along(ey, ez),
            device_id_type=MESH,
        ).start()

    def arrived(dy, dz, h):
        block = half(dy, dz, h)
        pltpu.make_async_copy(block, block, tab_recv.at[h * 16 + dy * 4 + dz]).wait()

    def mirrored(e):
        return lax.rem(e + core * (4 - 2 * e), 4)

    order = [mirrored(e) for e in (1, 3, 2)]
    for e in order:
        pass_on(0, 0, 0, 0, e)
        pass_on(0, 0, 1, e, 0)
    for e in order:
        pass_on(0, 0, 0, e, 0)
        pass_on(0, 0, 1, 0, e)

    for s in (0, HALF):
        for g in range(1, 8):
            pltpu.make_async_remote_copy(
                src_ref=ids_send.at[s + g],
                dst_ref=ids_recv.at[s + g],
                send_sem=ids_ssem,
                recv_sem=ids_rsem,
                device_id=member(s, g),
                device_id_type=MESH,
            ).start()
        ids_recv[s] = ids_send[s]

    for d in order:
        arrived(0, d, 0)
        for e in order:
            pass_on(0, d, 0, e, 0)
        arrived(d, 0, 1)
        for e in order:
            pass_on(d, 0, 1, 0, e)
    part = ids_recv.at[pl.ds(0, 14)]
    pltpu.make_async_copy(part, part, ids_rsem).wait()
    vec_same = iota((LEAF, LEAF), 0) % NVEC == iota((LEAF, LEAF), 1) % NVEC
    cluster_row = (iota((LEAF, LEAF), 0) // NVEC).astype(F32)
    left = iota((1, LEAF), 1) < LEAF // 2

    def make_mask(p, carry):
        for s in (0, HALF):
            for a in range(4):
                wanted = jnp.where(left, ids_recv[s + 2 * a, p], ids_recv[s + 2 * a + 1, p])
                pick = jnp.where(vec_same & (cluster_row == wanted), 1.0, 0.0)
                masks[s + p, :, a * LEAF : (a + 1) * LEAF] = pick.astype(BF16)
        return carry

    lax.fori_loop(0, HALF, make_mask, 0)

    for d in order:
        arrived(d, 0, 0)
        arrived(0, d, 1)
    for d in order:
        for e in order:
            arrived(d, e, 0)
            arrived(d, e, 1)

    loads[3].wait()
    lane = iota((NVEC, LEAF), 1)

    def gather(c, carry):
        got = jnp.zeros((NVEC, LEAF), F32)
        for n in range(LEAF):
            row = rows_ref[c, n] & (TILES * LEAF - 1)
            tile = table[lax.shift_right_logical(row, 7)].astype(F32)
            got = jnp.where(lane == n, pltpu.roll(tile, (n - row) & (LEAF - 1), axis=1), got)
        bound[c] = got.astype(BF16)
        return carry

    lax.fori_loop(0, CLUSTERS, gather, 0)

    for load in loads[4:7]:
        load.wait()
    to_smem.wait()
    same = iota((8 * NVEC, 8 * RANK), 0) // NVEC == iota((8 * NVEC, 8 * RANK), 1) // RANK

    def far(devs):
        pairs = [
            jnp.clip(idx_sm[j, dev[0] * 16 + dev[1]], 0, FAR - 1) for dev in devs for j in range(SLOTS)
        ]
        lhs = jnp.concatenate([bound[fsrc_ref[q]] for q in pairs], axis=0)
        v = jnp.concatenate([fv_vm[q] for q in pairs], axis=0)
        u = jnp.concatenate([fu_vm[q] for q in pairs], axis=0)
        coeff = lax.dot_general(lhs, v, NT, preferred_element_type=F32)
        coeff = jnp.where(same, coeff, 0.0).astype(BF16)
        term = jnp.dot(coeff, u, preferred_element_type=F32).astype(BF16)
        return term.reshape(2, SLOTS * NVEC, LEAF)

    def members():
        for h in range(4):
            for s in (0, HALF):
                yield s, h, mirrored(h if s == 0 else (4 - h) % 4) * 2

    def far_step(p, carry):
        for s, h, first in members():
            term = far([owner(s >= HALF, first + c, p) for c in range(2)])
            if h == 0:
                recv[s + p, 0] = term[0]
                send[s + p, 1] = term[1]
            else:
                send[s + p, pl.ds(first, 2)] = term
        for s, h, first in members():
            for c in range(2):
                if h + c == 0:
                    continue
                g = first + c
                pltpu.make_async_remote_copy(
                    src_ref=send.at[s + p, g],
                    dst_ref=recv.at[s + p, g],
                    send_sem=send_sem,
                    recv_sem=recv_sem.at[s + p],
                    device_id=member(s, g),
                    device_id_type=MESH,
                ).start()
        return carry

    lax.fori_loop(0, HALF, far_step, 0)

    def line_sum(s, p):
        part = recv.at[s + p, pl.ds(1, 7)]
        pltpu.make_async_copy(part, part, recv_sem.at[s + p]).wait()
        block = recv[s + p].reshape(8 * SLOTS * NVEC, LEAF)
        return jnp.dot(masks[s + p], block, preferred_element_type=F32)

    def merge(s, p):
        wide_send[s + p] = line_sum(s, p)
        pltpu.make_async_remote_copy(
            src_ref=wide_send.at[s + p],
            dst_ref=wide_recv.at[s + p],
            send_sem=wide_ssem,
            recv_sem=wide_rsem.at[s + p],
            device_id=owner(s >= HALF, 0, p),
            device_id_type=MESH,
        ).start()

    def merge_step(p, carry):
        merge(0, p)
        merge(HALF, p)
        return carry

    lax.fori_loop(0, SPLIT, merge_step, 0)

    for load in loads[7:]:
        load.wait()

    def near(g, carry):
        first = g * 8
        for i in range(8):
            term = lax.dot_general(bound[nsrc_ref[first + i]], near_vm[first + i], NT, preferred_element_type=F32)
            high = term.astype(BF16)
            nterm_hi[first + i] = high
            nterm_lo[first + i] = (term - high.astype(F32)).astype(BF16)
        return carry

    lax.fori_loop(0, NEAR // 8, near, 0)

    rows = 3 * CLUSTERS * NVEC
    named = (noff_ref[...] * CLUSTERS + nclu_ref[...]).astype(F32).astype(BF16)
    named = jnp.broadcast_to(named, (16, NEAR))
    vec_row = iota((rows, 256), 0) % NVEC == iota((rows, 256), 1) % NVEC
    target_row = (iota((rows, 256), 0) // NVEC).astype(F32)
    nsum[...] = jnp.zeros_like(nsum)

    def near_sum(g, carry):
        first = g * 16
        spread = (iota((NEAR, 256), 0) == first + iota((NEAR, 256), 1) // NVEC).astype(F32).astype(BF16)
        wanted = jnp.dot(named, spread, preferred_element_type=F32)[0:1, :]
        pick = jnp.where(vec_row & (target_row == wanted), 1.0, 0.0).astype(BF16)
        high = nterm_hi[pl.ds(first, 16)].reshape(256, LEAF)
        low = nterm_lo[pl.ds(first, 16)].reshape(256, LEAF)
        total = jnp.dot(pick, high, preferred_element_type=F32) + jnp.dot(pick, low, preferred_element_type=F32)
        nsum[...] += total.reshape(3 * CLUSTERS, NVEC, LEAF)
        return carry

    lax.fori_loop(0, NEAR // 16, near_sum, 0)

    me = clu * 16 + vol
    before, after = lax.rem(me + NDEV - 1, NDEV), lax.rem(me + 1, NDEV)
    near_copies = []
    for i, (block, to) in enumerate(((0, before), (2, after))):
        copy = pltpu.make_async_remote_copy(
            src_ref=nsum.at[pl.ds(block * CLUSTERS, CLUSTERS)],
            dst_ref=nrecv.at[i],
            send_sem=near_ssem.at[i],
            recv_sem=near_rsem.at[i],
            device_id=(lax.div(to, 16), lax.rem(to, 16)),
            device_id_type=MESH,
        )
        copy.start()
        near_copies.append(copy)

    lax.fori_loop(SPLIT, HALF - 1, merge_step, 0)
    merge(HALF, HALF - 1)
    total = line_sum(0, HALF - 1) + nsum[pl.ds(CLUSTERS, CLUSTERS)].reshape(CLUSTERS * NVEC, LEAF)
    for copy in near_copies:
        copy.wait()
    total += (nrecv[0] + nrecv[1]).reshape(CLUSTERS * NVEC, LEAF)
    for p in range(HALF):
        for s in (0, HALF):
            if s + p != HALF - 1:
                part = wide_recv.at[s + p]
                pltpu.make_async_copy(part, part, wide_rsem.at[s + p]).wait()
                total += wide_recv[s + p]
    out_ref[...] = total.reshape(CLUSTERS, NVEC, LEAF)

    sent = table.at[pl.ds(0, 240)]
    pltpu.make_async_copy(sent, sent, tab_send).wait()
    sent = ids_recv.at[pl.ds(0, 14)]
    pltpu.make_async_copy(sent, sent, ids_ssem).wait()
    sent = send.at[pl.ds(0, 14)]
    pltpu.make_async_copy(sent, sent, send_sem).wait()
    sent = wide_send.at[pl.ds(0, 15)]
    pltpu.make_async_copy(sent, sent, wide_ssem).wait()


def body(
    volume_field,
    trace_rows,
    near_block,
    near_source,
    near_offset,
    near_cluster,
    far_v,
    far_u,
    far_source,
    far_owner,
    far_cluster,
):
    vmem = pl.BlockSpec(memory_space=pltpu.VMEM)
    hbm = pl.BlockSpec(memory_space=pltpu.HBM)
    dma = pltpu.SemaphoreType.DMA
    return pl.pallas_call(
        kernel,
        out_shape=jax.ShapeDtypeStruct((CLUSTERS, NVEC, LEAF), F32),
        in_specs=[hbm] * 11,
        out_specs=vmem,
        scratch_shapes=[
            pltpu.VMEM((NVEC, TILES // 16 * LEAF), BF16),
            pltpu.SMEM((CLUSTERS, LEAF), jnp.int32),
            pltpu.SMEM((NEAR,), jnp.int32),
            pltpu.VMEM((1, NEAR), jnp.int32),
            pltpu.VMEM((1, NEAR), jnp.int32),
            pltpu.SMEM((FAR,), jnp.int32),
            pltpu.VMEM((1, FAR), jnp.int32),
            pltpu.VMEM((1, FAR), jnp.int32),
            pltpu.VMEM((TILES, NVEC, LEAF), BF16),
            pltpu.VMEM((NEAR, LEAF, LEAF), BF16),
            pltpu.VMEM((FAR, RANK, LEAF), BF16),
            pltpu.VMEM((FAR, RANK, LEAF), BF16),
            pltpu.VMEM((CLUSTERS, NVEC, LEAF), BF16),
            pltpu.VMEM((STEPS, 8, SLOTS * NVEC, LEAF), BF16),
            pltpu.VMEM((STEPS, 8, SLOTS * NVEC, LEAF), BF16),
            pltpu.VMEM((STEPS, LEAF, LEAF), F32),
            pltpu.VMEM((STEPS, LEAF, LEAF), F32),
            pltpu.VMEM((8, NDEV), jnp.int32),
            pltpu.SMEM((8, NDEV), jnp.int32),
            pltpu.VMEM((NDEV, 1, LEAF), F32),
            pltpu.VMEM((STEPS, HALF, 1, LEAF), F32),
            pltpu.VMEM((STEPS, HALF, 1, LEAF), F32),
            pltpu.VMEM((STEPS, LEAF, 8 * SLOTS * NVEC), BF16),
            pltpu.VMEM((NEAR, NVEC, LEAF), BF16),
            pltpu.VMEM((NEAR, NVEC, LEAF), BF16),
            pltpu.VMEM((3 * CLUSTERS, NVEC, LEAF), F32),
            pltpu.VMEM((2, CLUSTERS, NVEC, LEAF), F32),
            dma((11,)),
            dma,
            dma,
            dma((32,)),
            dma,
            dma,
            dma,
            dma((STEPS,)),
            dma,
            dma((STEPS,)),
            dma((2,)),
            dma((2,)),
        ],
        compiler_params=pltpu.CompilerParams(
            collective_id=0, has_side_effects=True, vmem_limit_bytes=40 * 2**20
        ),
        cost_estimate=pl.CostEstimate(flops=2 * 10**8, bytes_accessed=9 * 2**20, transcendentals=0),
    )(
        *(pltpu.with_memory_space_constraint(a, pltpu.HBM) for a in (
        volume_field,
        trace_rows,
        near_source,
        near_offset.reshape(1, NEAR),
        near_cluster.reshape(1, NEAR),
        far_source,
        far_owner.reshape(1, FAR),
        far_cluster.reshape(1, FAR),
        near_block,
        far_v,
        far_u,
    )))


def solution(mesh):
    both = ("clu", "vol")
    return jax.shard_map(
        body,
        mesh=mesh,
        in_specs=(
            P(None, both),
            P(both, None),
            P(both, None, None),
            P(both),
            P(both),
            P(both),
            P(both, None, None),
            P(both, None, None),
            P(both),
            P(both, None),
            P(both),
        ),
        out_specs=P(both, None, None),
        check_vma=False,
    )
```

```python
import jax
import jax.numpy as jnp
from jax import lax
from jax.experimental import pallas as pl
from jax.experimental.pallas import tpu as pltpu
from jax.sharding import PartitionSpec as P

MESH = pl.DeviceIdType.MESH
F32 = jnp.float32
BF16 = jnp.bfloat16
NT = (((1,), (1,)), ((), ()))

LEAF = 128
NVEC = 16
NDEV = 128
CLUSTERS = 8
SLOTS = 4
NEAR = 128
FAR = 256
RANK = 32
STEPS = 16
LAG = 4
HALF = 8
TILES = 256


def iota(shape, dim):
    return lax.broadcasted_iota(jnp.int32, shape, dim)


def place():
    clu, vol = lax.axis_index("clu"), lax.axis_index("vol")
    return lax.div(clu, 2), lax.rem(clu, 2), lax.div(vol, 4), lax.rem(vol, 4)


def at(dx, dcore, dy, dz):
    x, core, y, z = place()
    clu = lax.rem(x + dx, 4) * 2 + lax.rem(core + dcore, 2)
    return clu, lax.rem(y + dy, 4) * 4 + lax.rem(z + dz, 4)


def member(s, g):
    return at(lax.div(g, 2), lax.rem(g, 2), 0, 0) if s < HALF else at(0, lax.rem(g, 2), lax.div(g, 2), 0)


def offset(along_y, p):
    if along_y:
        return lax.rem(lax.div(p, 2) + 1, 4), 1 + 2 * lax.rem(p, 2)
    return lax.rem(p + 1, 4), 2 - 2 * lax.div(p, 4)


def owner(along_y, g, p):
    d, dz = offset(along_y, p)
    return at(d, lax.rem(g, 2), lax.div(g, 2), dz) if along_y else at(lax.div(g, 2), lax.rem(g, 2), d, dz)


def kernel(
    vol_hbm,
    rows_hbm,
    nsrc_hbm,
    noff_hbm,
    nclu_hbm,
    fsrc_hbm,
    fown_hbm,
    fclu_hbm,
    near_hbm,
    fv_hbm,
    fu_hbm,
    out_ref,
    vol_ref,
    rows_ref,
    nsrc_ref,
    noff_ref,
    nclu_ref,
    fsrc_ref,
    fown_ref,
    fclu_ref,
    table,
    near_vm,
    fv_vm,
    fu_vm,
    bound,
    send,
    recv,
    wide_send,
    wide_recv,
    idx_vm,
    idx_sm,
    ids_all,
    ids_send,
    ids_recv,
    masks,
    nterm_hi,
    nterm_lo,
    nsum,
    nrecv,
    load_sem,
    idx_sem,
    tab_send,
    tab_recv,
    ids_ssem,
    ids_rsem,
    send_sem,
    recv_sem,
    wide_ssem,
    wide_rsem,
    near_ssem,
    near_rsem,
):
    x, core, y, z = place()
    clu, vol = lax.axis_index("clu"), lax.axis_index("vol")

    barrier = pltpu.get_barrier_semaphore()

    def along_clu(k):
        return lax.rem(clu + k, 8), vol

    def along(ey, ez):
        return clu, lax.rem(y + ey, 4) * 4 + lax.rem(z + ez, 4)

    near_by = [along_clu(k) for k in range(1, 8)]
    near_by += [at(0, c, e, 0) for c in range(2) for e in range(1, 4)] + [along(0, e) for e in range(1, 4)]
    for dev in near_by:
        pl.semaphore_signal(barrier, inc=1, device_id=dev, device_id_type=MESH)

    pairs = (
        (vol_hbm, vol_ref),
        (fown_hbm, fown_ref),
        (fclu_hbm, fclu_ref),
        (rows_hbm, rows_ref),
        (fsrc_hbm, fsrc_ref),
        (fv_hbm, fv_vm),
        (fu_hbm, fu_vm),
        (nsrc_hbm, nsrc_ref),
        (noff_hbm, noff_ref),
        (nclu_hbm, nclu_ref),
        (near_hbm, near_vm),
    )
    loads = [pltpu.make_async_copy(a, b, load_sem.at[i]) for i, (a, b) in enumerate(pairs)]
    for load in loads:
        load.start()
    for load in loads[:3]:
        load.wait()

    base = vol * 16
    for hi in range(16):
        table[base + hi] = vol_ref[:, hi * LEAF : (hi + 1) * LEAF]

    owns = iota((NDEV, FAR), 0) == fown_ref[...]
    upto = (iota((FAR, FAR), 0) <= iota((FAR, FAR), 1)).astype(F32).astype(BF16)
    count = jnp.dot(owns.astype(F32).astype(BF16), upto, preferred_element_type=F32)
    number = iota((16, FAR), 1).astype(F32).astype(BF16)
    clusters = fclu_ref[...].astype(F32) + 1.0
    slot_of_lane = (iota((NDEV, LEAF), 1) // NVEC) % SLOTS
    ids = jnp.zeros((NDEV, LEAF), F32)
    for j in range(SLOTS):
        chosen = jnp.where(owns & (count == float(j + 1)), 1.0, 0.0)
        found = lax.dot_general(number, chosen.astype(BF16), NT, preferred_element_type=F32)
        idx_vm[j : j + 1, :] = found[0:1, :].astype(jnp.int32)
        target = jnp.sum(chosen * clusters, axis=1, keepdims=True) - 1.0
        ids = jnp.where(slot_of_lane == j, target, ids)
    ids_all[...] = ids.reshape(NDEV, 1, LEAF)
    for s in (0, HALF):
        for g in range(8):

            def ids_row(p, carry, s=s, g=g):
                dev = owner(s >= HALF, g, p)
                ids_send[s + g, p] = ids_all[dev[0] * 16 + dev[1]]
                return carry

            lax.fori_loop(0, HALF, ids_row, 0, unroll=4)
    to_smem = pltpu.make_async_copy(idx_vm, idx_sm, idx_sem)
    to_smem.start()

    pl.semaphore_wait(barrier, len(near_by))

    def half(dy, dz, h):
        owner = lax.rem(y + 4 - dy, 4) * 4 + lax.rem(z + 4 - dz, 4)
        return table.at[pl.ds(owner * 16 + h * 8, 8)]

    def pass_on(dy, dz, h, ey, ez):
        block = half(dy, dz, h)
        pltpu.make_async_remote_copy(
            src_ref=block,
            dst_ref=block,
            send_sem=tab_send,
            recv_sem=tab_recv.at[h * 16 + (dy + ey) * 4 + dz + ez],
            device_id=along(ey, ez),
            device_id_type=MESH,
        ).start()

    def arrived(dy, dz, h):
        block = half(dy, dz, h)
        pltpu.make_async_copy(block, block, tab_recv.at[h * 16 + dy * 4 + dz]).wait()

    def mirrored(e):
        return lax.rem(e + core * (4 - 2 * e), 4)

    order = [mirrored(e) for e in (1, 3, 2)]
    for e in order:
        pass_on(0, 0, 0, 0, e)
        pass_on(0, 0, 1, e, 0)
    for e in order:
        pass_on(0, 0, 0, e, 0)
        pass_on(0, 0, 1, 0, e)

    for s in (0, HALF):
        for g in range(1, 8):
            pltpu.make_async_remote_copy(
                src_ref=ids_send.at[s + g],
                dst_ref=ids_recv.at[s + g],
                send_sem=ids_ssem,
                recv_sem=ids_rsem,
                device_id=member(s, g),
                device_id_type=MESH,
            ).start()
        ids_recv[s] = ids_send[s]

    for d in order:
        arrived(0, d, 0)
        for e in order:
            pass_on(0, d, 0, e, 0)
        arrived(d, 0, 1)
        for e in order:
            pass_on(d, 0, 1, 0, e)
    part = ids_recv.at[pl.ds(0, 14)]
    pltpu.make_async_copy(part, part, ids_rsem).wait()
    vec_same = iota((LEAF, LEAF), 0) % NVEC == iota((LEAF, LEAF), 1) % NVEC
    cluster_row = (iota((LEAF, LEAF), 0) // NVEC).astype(F32)
    left = iota((1, LEAF), 1) < LEAF // 2

    def make_mask(p, carry):
        for s in (0, HALF):
            for a in range(4):
                wanted = jnp.where(left, ids_recv[s + 2 * a, p], ids_recv[s + 2 * a + 1, p])
                pick = jnp.where(vec_same & (cluster_row == wanted), 1.0, 0.0)
                masks[s + p, :, a * LEAF : (a + 1) * LEAF] = pick.astype(BF16)
        return carry

    lax.fori_loop(0, HALF, make_mask, 0)

    for d in order:
        arrived(d, 0, 0)
        arrived(0, d, 1)
    for d in order:
        for e in order:
            arrived(d, e, 0)
            arrived(d, e, 1)

    loads[3].wait()
    lane = iota((NVEC, LEAF), 1)

    def gather(c, carry):
        got = jnp.zeros((NVEC, LEAF), F32)
        for n in range(LEAF):
            row = rows_ref[c, n] & (TILES * LEAF - 1)
            tile = table[lax.shift_right_logical(row, 7)].astype(F32)
            got = jnp.where(lane == n, pltpu.roll(tile, (n - row) & (LEAF - 1), axis=1), got)
        bound[c] = got.astype(BF16)
        return carry

    lax.fori_loop(0, CLUSTERS, gather, 0)

    for load in loads[4:7]:
        load.wait()
    to_smem.wait()
    same = iota((8 * NVEC, 8 * RANK), 0) // NVEC == iota((8 * NVEC, 8 * RANK), 1) // RANK

    def far(devs):
        pairs = [
            jnp.clip(idx_sm[j, dev[0] * 16 + dev[1]], 0, FAR - 1) for dev in devs for j in range(SLOTS)
        ]
        lhs = jnp.concatenate([bound[fsrc_ref[q]] for q in pairs], axis=0)
        v = jnp.concatenate([fv_vm[q] for q in pairs], axis=0)
        u = jnp.concatenate([fu_vm[q] for q in pairs], axis=0)
        coeff = lax.dot_general(lhs, v, NT, preferred_element_type=F32)
        coeff = jnp.where(same, coeff, 0.0).astype(BF16)
        term = jnp.dot(coeff, u, preferred_element_type=F32).astype(BF16)
        return term.reshape(2, SLOTS * NVEC, LEAF)

    def members():
        for h in range(4):
            for s in (0, HALF):
                yield s, h, mirrored(h if s == 0 else (4 - h) % 4) * 2

    def far_step(p, carry):
        for s, h, first in members():
            term = far([owner(s >= HALF, first + c, p) for c in range(2)])
            if h == 0:
                recv[s + p, 0] = term[0]
                send[s + p, 1] = term[1]
            else:
                send[s + p, pl.ds(first, 2)] = term
        for s, h, first in members():
            for c in range(2):
                if h + c == 0:
                    continue
                g = first + c
                pltpu.make_async_remote_copy(
                    src_ref=send.at[s + p, g],
                    dst_ref=recv.at[s + p, g],
                    send_sem=send_sem,
                    recv_sem=recv_sem.at[s + p],
                    device_id=member(s, g),
                    device_id_type=MESH,
                ).start()
        return carry

    def line_sum(s, p):
        part = recv.at[s + p, pl.ds(1, 7)]
        pltpu.make_async_copy(part, part, recv_sem.at[s + p]).wait()
        block = recv[s + p].reshape(8 * SLOTS * NVEC, LEAF)
        return jnp.dot(masks[s + p], block, preferred_element_type=F32)

    def merge(s, p):
        wide_send[s + p] = line_sum(s, p)
        pltpu.make_async_remote_copy(
            src_ref=wide_send.at[s + p],
            dst_ref=wide_recv.at[s + p],
            send_sem=wide_ssem,
            recv_sem=wide_rsem.at[s + p],
            device_id=owner(s >= HALF, 0, p),
            device_id_type=MESH,
        ).start()

    def merge_step(p, carry):
        merge(0, p)
        merge(HALF, p)
        return carry

    def near(g, carry):
        first = g * 8
        for i in range(8):
            term = lax.dot_general(bound[nsrc_ref[first + i]], near_vm[first + i], NT, preferred_element_type=F32)
            high = term.astype(BF16)
            nterm_hi[first + i] = high
            nterm_lo[first + i] = (term - high.astype(F32)).astype(BF16)
        return carry

    for load in loads[7:]:
        load.wait()
    rows = 3 * CLUSTERS * NVEC
    named = (noff_ref[...] * CLUSTERS + nclu_ref[...]).astype(F32).astype(BF16)
    named = jnp.broadcast_to(named, (16, NEAR))
    vec_row = iota((rows, 256), 0) % NVEC == iota((rows, 256), 1) % NVEC
    target_row = (iota((rows, 256), 0) // NVEC).astype(F32)

    def near_sum(g, carry):
        first = g * 16
        spread = (iota((NEAR, 256), 0) == first + iota((NEAR, 256), 1) // NVEC).astype(F32).astype(BF16)
        wanted = jnp.dot(named, spread, preferred_element_type=F32)[0:1, :]
        pick = jnp.where(vec_row & (target_row == wanted), 1.0, 0.0).astype(BF16)
        high = nterm_hi[pl.ds(first, 16)].reshape(256, LEAF)
        low = nterm_lo[pl.ds(first, 16)].reshape(256, LEAF)
        total = jnp.dot(pick, high, preferred_element_type=F32) + jnp.dot(pick, low, preferred_element_type=F32)
        nsum[...] += total.reshape(3 * CLUSTERS, NVEC, LEAF)
        return carry

    def near_piece(q):
        near(2 * q, 0)
        near(2 * q + 1, 0)
        near_sum(q, 0)

    def both_steps(p, carry):
        far_step(p, carry)
        near_piece(p - LAG)
        return merge_step(p - LAG, carry)

    lax.fori_loop(0, LAG, far_step, 0)
    nsum[...] = jnp.zeros_like(nsum)
    lax.fori_loop(LAG, HALF, both_steps, 0)

    def late_steps(p, carry):
        near_piece(p)
        return merge_step(p, carry)

    lax.fori_loop(HALF - LAG, HALF - 1, late_steps, 0)
    near_piece(HALF - 1)
    me = clu * 16 + vol
    before, after = lax.rem(me + NDEV - 1, NDEV), lax.rem(me + 1, NDEV)
    near_copies = []
    for i, (block, to) in enumerate(((0, before), (2, after))):
        copy = pltpu.make_async_remote_copy(
            src_ref=nsum.at[pl.ds(block * CLUSTERS, CLUSTERS)],
            dst_ref=nrecv.at[i],
            send_sem=near_ssem.at[i],
            recv_sem=near_rsem.at[i],
            device_id=(lax.div(to, 16), lax.rem(to, 16)),
            device_id_type=MESH,
        )
        copy.start()
        near_copies.append(copy)

    merge(HALF, HALF - 1)
    total = line_sum(0, HALF - 1) + nsum[pl.ds(CLUSTERS, CLUSTERS)].reshape(CLUSTERS * NVEC, LEAF)
    for copy in near_copies:
        copy.wait()
    total += (nrecv[0] + nrecv[1]).reshape(CLUSTERS * NVEC, LEAF)
    for p in range(HALF):
        for s in (0, HALF):
            if s + p != HALF - 1:
                part = wide_recv.at[s + p]
                pltpu.make_async_copy(part, part, wide_rsem.at[s + p]).wait()
                total += wide_recv[s + p]
    out_ref[...] = total.reshape(CLUSTERS, NVEC, LEAF)

    sent = table.at[pl.ds(0, 240)]
    pltpu.make_async_copy(sent, sent, tab_send).wait()
    sent = ids_recv.at[pl.ds(0, 14)]
    pltpu.make_async_copy(sent, sent, ids_ssem).wait()
    sent = send.at[pl.ds(0, 14)]
    pltpu.make_async_copy(sent, sent, send_sem).wait()
    sent = wide_send.at[pl.ds(0, 15)]
    pltpu.make_async_copy(sent, sent, wide_ssem).wait()


def body(
    volume_field,
    trace_rows,
    near_block,
    near_source,
    near_offset,
    near_cluster,
    far_v,
    far_u,
    far_source,
    far_owner,
    far_cluster,
):
    vmem = pl.BlockSpec(memory_space=pltpu.VMEM)
    hbm = pl.BlockSpec(memory_space=pltpu.HBM)
    dma = pltpu.SemaphoreType.DMA
    return pl.pallas_call(
        kernel,
        out_shape=jax.ShapeDtypeStruct((CLUSTERS, NVEC, LEAF), F32),
        in_specs=[hbm] * 11,
        out_specs=vmem,
        scratch_shapes=[
            pltpu.VMEM((NVEC, TILES // 16 * LEAF), BF16),
            pltpu.SMEM((CLUSTERS, LEAF), jnp.int32),
            pltpu.SMEM((NEAR,), jnp.int32),
            pltpu.VMEM((1, NEAR), jnp.int32),
            pltpu.VMEM((1, NEAR), jnp.int32),
            pltpu.SMEM((FAR,), jnp.int32),
            pltpu.VMEM((1, FAR), jnp.int32),
            pltpu.VMEM((1, FAR), jnp.int32),
            pltpu.VMEM((TILES, NVEC, LEAF), BF16),
            pltpu.VMEM((NEAR, LEAF, LEAF), BF16),
            pltpu.VMEM((FAR, RANK, LEAF), BF16),
            pltpu.VMEM((FAR, RANK, LEAF), BF16),
            pltpu.VMEM((CLUSTERS, NVEC, LEAF), BF16),
            pltpu.VMEM((STEPS, 8, SLOTS * NVEC, LEAF), BF16),
            pltpu.VMEM((STEPS, 8, SLOTS * NVEC, LEAF), BF16),
            pltpu.VMEM((STEPS, LEAF, LEAF), F32),
            pltpu.VMEM((STEPS, LEAF, LEAF), F32),
            pltpu.VMEM((8, NDEV), jnp.int32),
            pltpu.SMEM((8, NDEV), jnp.int32),
            pltpu.VMEM((NDEV, 1, LEAF), F32),
            pltpu.VMEM((STEPS, HALF, 1, LEAF), F32),
            pltpu.VMEM((STEPS, HALF, 1, LEAF), F32),
            pltpu.VMEM((STEPS, LEAF, 8 * SLOTS * NVEC), BF16),
            pltpu.VMEM((NEAR, NVEC, LEAF), BF16),
            pltpu.VMEM((NEAR, NVEC, LEAF), BF16),
            pltpu.VMEM((3 * CLUSTERS, NVEC, LEAF), F32),
            pltpu.VMEM((2, CLUSTERS, NVEC, LEAF), F32),
            dma((11,)),
            dma,
            dma,
            dma((32,)),
            dma,
            dma,
            dma,
            dma((STEPS,)),
            dma,
            dma((STEPS,)),
            dma((2,)),
            dma((2,)),
        ],
        compiler_params=pltpu.CompilerParams(
            collective_id=0, has_side_effects=True, vmem_limit_bytes=40 * 2**20
        ),
        cost_estimate=pl.CostEstimate(flops=2 * 10**8, bytes_accessed=9 * 2**20, transcendentals=0),
    )(
        *(pltpu.with_memory_space_constraint(a, pltpu.HBM) for a in (
        volume_field,
        trace_rows,
        near_source,
        near_offset.reshape(1, NEAR),
        near_cluster.reshape(1, NEAR),
        far_source,
        far_owner.reshape(1, FAR),
        far_cluster.reshape(1, FAR),
        near_block,
        far_v,
        far_u,
    )))


def solution(mesh):
    both = ("clu", "vol")
    return jax.shard_map(
        body,
        mesh=mesh,
        in_specs=(
            P(None, both),
            P(both, None),
            P(both, None, None),
            P(both),
            P(both),
            P(both),
            P(both, None, None),
            P(both, None, None),
            P(both),
            P(both, None),
            P(both),
        ),
        out_specs=P(both, None, None),
        check_vma=False,
    )
```

```python
import jax
import jax.numpy as jnp
from jax import lax
from jax.experimental import pallas as pl
from jax.experimental.pallas import tpu as pltpu
from jax.sharding import PartitionSpec as P

MESH = pl.DeviceIdType.MESH
F32 = jnp.float32
BF16 = jnp.bfloat16
NT = (((1,), (1,)), ((), ()))

LEAF = 128
NVEC = 16
NDEV = 128
CLUSTERS = 8
SLOTS = 4
NEAR = 128
FAR = 256
RANK = 32
STEPS = 16
LAG = 4
HALF = 8
TILES = 256


def iota(shape, dim):
    return lax.broadcasted_iota(jnp.int32, shape, dim)


def place():
    clu, vol = lax.axis_index("clu"), lax.axis_index("vol")
    return lax.div(clu, 2), lax.rem(clu, 2), lax.div(vol, 4), lax.rem(vol, 4)


def at(dx, dcore, dy, dz):
    x, core, y, z = place()
    clu = lax.rem(x + dx, 4) * 2 + lax.rem(core + dcore, 2)
    return clu, lax.rem(y + dy, 4) * 4 + lax.rem(z + dz, 4)


def member(s, g):
    return at(lax.div(g, 2), lax.rem(g, 2), 0, 0) if s < HALF else at(0, lax.rem(g, 2), lax.div(g, 2), 0)


def offset(along_y, p):
    if along_y:
        return lax.rem(lax.div(p, 2) + 1, 4), 1 + 2 * lax.rem(p, 2)
    return lax.rem(p + 1, 4), 2 - 2 * lax.div(p, 4)


def owner(along_y, g, p):
    d, dz = offset(along_y, p)
    return at(d, lax.rem(g, 2), lax.div(g, 2), dz) if along_y else at(lax.div(g, 2), lax.rem(g, 2), d, dz)


def kernel(
    vol_hbm,
    rows_hbm,
    nsrc_hbm,
    noff_hbm,
    nclu_hbm,
    fsrc_hbm,
    fown_hbm,
    fclu_hbm,
    near_hbm,
    fv_hbm,
    fu_hbm,
    out_ref,
    vol_ref,
    rows_ref,
    nsrc_ref,
    noff_ref,
    nclu_ref,
    fsrc_ref,
    fown_ref,
    fclu_ref,
    table,
    near_vm,
    fv_vm,
    fu_vm,
    bound,
    send,
    recv,
    wide_send,
    wide_recv,
    idx_vm,
    idx_sm,
    ids_all,
    ids_send,
    ids_recv,
    masks,
    nterm_hi,
    nterm_lo,
    nsum,
    nrecv,
    load_sem,
    idx_sem,
    tab_send,
    tab_recv,
    ids_ssem,
    ids_rsem,
    send_sem,
    recv_sem,
    wide_ssem,
    wide_rsem,
    near_ssem,
    near_rsem,
):
    x, core, y, z = place()
    clu, vol = lax.axis_index("clu"), lax.axis_index("vol")

    barrier = pltpu.get_barrier_semaphore()

    def along_clu(k):
        return lax.rem(clu + k, 8), vol

    def along(ey, ez):
        return clu, lax.rem(y + ey, 4) * 4 + lax.rem(z + ez, 4)

    near_by = [along_clu(k) for k in range(1, 8)]
    near_by += [at(0, c, e, 0) for c in range(2) for e in range(1, 4)] + [along(0, e) for e in range(1, 4)]
    for dev in near_by:
        pl.semaphore_signal(barrier, inc=1, device_id=dev, device_id_type=MESH)

    pairs = (
        (vol_hbm, vol_ref),
        (fown_hbm, fown_ref),
        (fclu_hbm, fclu_ref),
        (rows_hbm, rows_ref),
        (fsrc_hbm, fsrc_ref),
        (fv_hbm, fv_vm),
        (fu_hbm, fu_vm),
        (nsrc_hbm, nsrc_ref),
        (noff_hbm, noff_ref),
        (nclu_hbm, nclu_ref),
        (near_hbm, near_vm),
    )
    loads = [pltpu.make_async_copy(a, b, load_sem.at[i]) for i, (a, b) in enumerate(pairs)]
    for load in loads:
        load.start()
    for load in loads[:3]:
        load.wait()

    base = vol * 16
    for hi in range(16):
        table[base + hi] = vol_ref[:, hi * LEAF : (hi + 1) * LEAF]

    owns = iota((NDEV, FAR), 0) == fown_ref[...]
    upto = (iota((FAR, FAR), 0) <= iota((FAR, FAR), 1)).astype(F32).astype(BF16)
    count = jnp.dot(owns.astype(F32).astype(BF16), upto, preferred_element_type=F32)
    number = iota((16, FAR), 1).astype(F32).astype(BF16)
    clusters = fclu_ref[...].astype(F32) + 1.0
    slot_of_lane = (iota((NDEV, LEAF), 1) // NVEC) % SLOTS
    ids = jnp.zeros((NDEV, LEAF), F32)
    for j in range(SLOTS):
        chosen = jnp.where(owns & (count == float(j + 1)), 1.0, 0.0)
        found = lax.dot_general(number, chosen.astype(BF16), NT, preferred_element_type=F32)
        idx_vm[j : j + 1, :] = found[0:1, :].astype(jnp.int32)
        target = jnp.sum(chosen * clusters, axis=1, keepdims=True) - 1.0
        ids = jnp.where(slot_of_lane == j, target, ids)
    ids_all[...] = ids.reshape(NDEV, 1, LEAF)
    for s in (0, HALF):
        for g in range(8):

            def ids_row(p, carry, s=s, g=g):
                dev = owner(s >= HALF, g, p)
                ids_send[s + g, p] = ids_all[dev[0] * 16 + dev[1]]
                return carry

            lax.fori_loop(0, HALF, ids_row, 0, unroll=4)
    to_smem = pltpu.make_async_copy(idx_vm, idx_sm, idx_sem)
    to_smem.start()

    pl.semaphore_wait(barrier, len(near_by))

    def half(dy, dz, h):
        owner = lax.rem(y + 4 - dy, 4) * 4 + lax.rem(z + 4 - dz, 4)
        return table.at[pl.ds(owner * 16 + h * 8, 8)]

    def pass_on(dy, dz, h, ey, ez):
        block = half(dy, dz, h)
        pltpu.make_async_remote_copy(
            src_ref=block,
            dst_ref=block,
            send_sem=tab_send,
            recv_sem=tab_recv.at[h * 16 + (dy + ey) * 4 + dz + ez],
            device_id=along(ey, ez),
            device_id_type=MESH,
        ).start()

    def arrived(dy, dz, h):
        block = half(dy, dz, h)
        pltpu.make_async_copy(block, block, tab_recv.at[h * 16 + dy * 4 + dz]).wait()

    def mirrored(e):
        return lax.rem(e + core * (4 - 2 * e), 4)

    order = [mirrored(e) for e in (2, 1, 3)]
    for e in order:
        pass_on(0, 0, 0, 0, e)
        pass_on(0, 0, 1, e, 0)
    for e in order:
        pass_on(0, 0, 0, e, 0)
        pass_on(0, 0, 1, 0, e)

    for s in (0, HALF):
        for g in range(1, 8):
            pltpu.make_async_remote_copy(
                src_ref=ids_send.at[s + g],
                dst_ref=ids_recv.at[s + g],
                send_sem=ids_ssem,
                recv_sem=ids_rsem,
                device_id=member(s, g),
                device_id_type=MESH,
            ).start()
        ids_recv[s] = ids_send[s]

    for d in order:
        arrived(0, d, 0)
        for e in order:
            pass_on(0, d, 0, e, 0)
        arrived(d, 0, 1)
        for e in order:
            pass_on(d, 0, 1, 0, e)
    part = ids_recv.at[pl.ds(0, 14)]
    pltpu.make_async_copy(part, part, ids_rsem).wait()
    vec_same = iota((LEAF, LEAF), 0) % NVEC == iota((LEAF, LEAF), 1) % NVEC
    cluster_row = (iota((LEAF, LEAF), 0) // NVEC).astype(F32)
    left = iota((1, LEAF), 1) < LEAF // 2

    def make_mask(p, carry):
        for s in (0, HALF):
            for a in range(4):
                wanted = jnp.where(left, ids_recv[s + 2 * a, p], ids_recv[s + 2 * a + 1, p])
                pick = jnp.where(vec_same & (cluster_row == wanted), 1.0, 0.0)
                masks[s + p, :, a * LEAF : (a + 1) * LEAF] = pick.astype(BF16)
        return carry

    lax.fori_loop(0, HALF, make_mask, 0)

    for d in order:
        arrived(d, 0, 0)
        arrived(0, d, 1)
    for d in order:
        for e in order:
            arrived(d, e, 0)
            arrived(d, e, 1)

    loads[3].wait()
    lane = iota((NVEC, LEAF), 1)

    def gather(c, carry):
        got = jnp.zeros((NVEC, LEAF), F32)
        for n in range(LEAF):
            row = rows_ref[c, n] & (TILES * LEAF - 1)
            tile = table[lax.shift_right_logical(row, 7)].astype(F32)
            got = jnp.where(lane == n, pltpu.roll(tile, (n - row) & (LEAF - 1), axis=1), got)
        bound[c] = got.astype(BF16)
        return carry

    lax.fori_loop(0, CLUSTERS, gather, 0)

    for load in loads[4:7]:
        load.wait()
    to_smem.wait()
    same = iota((8 * NVEC, 8 * RANK), 0) // NVEC == iota((8 * NVEC, 8 * RANK), 1) // RANK

    def far(devs):
        pairs = [
            jnp.clip(idx_sm[j, dev[0] * 16 + dev[1]], 0, FAR - 1) for dev in devs for j in range(SLOTS)
        ]
        lhs = jnp.concatenate([bound[fsrc_ref[q]] for q in pairs], axis=0)
        v = jnp.concatenate([fv_vm[q] for q in pairs], axis=0)
        u = jnp.concatenate([fu_vm[q] for q in pairs], axis=0)
        coeff = lax.dot_general(lhs, v, NT, preferred_element_type=F32)
        coeff = jnp.where(same, coeff, 0.0).astype(BF16)
        term = jnp.dot(coeff, u, preferred_element_type=F32).astype(BF16)
        return term.reshape(2, SLOTS * NVEC, LEAF)

    def members():
        for h in range(4):
            for s in (0, HALF):
                yield s, h, mirrored(h if s == 0 else (4 - h) % 4) * 2

    def far_step(p, carry):
        for s, h, first in members():
            term = far([owner(s >= HALF, first + c, p) for c in range(2)])
            if h == 0:
                recv[s + p, 0] = term[0]
                send[s + p, 1] = term[1]
            else:
                send[s + p, pl.ds(first, 2)] = term
        for s, h, first in members():
            for c in range(2):
                if h + c == 0:
                    continue
                g = first + c
                pltpu.make_async_remote_copy(
                    src_ref=send.at[s + p, g],
                    dst_ref=recv.at[s + p, g],
                    send_sem=send_sem,
                    recv_sem=recv_sem.at[s + p],
                    device_id=member(s, g),
                    device_id_type=MESH,
                ).start()
        return carry

    def line_sum(s, p):
        part = recv.at[s + p, pl.ds(1, 7)]
        pltpu.make_async_copy(part, part, recv_sem.at[s + p]).wait()
        block = recv[s + p].reshape(8 * SLOTS * NVEC, LEAF)
        return jnp.dot(masks[s + p], block, preferred_element_type=F32)

    def merge(s, p):
        wide_send[s + p] = line_sum(s, p)
        pltpu.make_async_remote_copy(
            src_ref=wide_send.at[s + p],
            dst_ref=wide_recv.at[s + p],
            send_sem=wide_ssem,
            recv_sem=wide_rsem.at[s + p],
            device_id=owner(s >= HALF, 0, p),
            device_id_type=MESH,
        ).start()

    def merge_step(p, carry):
        merge(0, p)
        merge(HALF, p)
        return carry

    def near(g, carry):
        first = g * 8
        for i in range(8):
            term = lax.dot_general(bound[nsrc_ref[first + i]], near_vm[first + i], NT, preferred_element_type=F32)
            high = term.astype(BF16)
            nterm_hi[first + i] = high
            nterm_lo[first + i] = (term - high.astype(F32)).astype(BF16)
        return carry

    for load in loads[7:]:
        load.wait()
    rows = 3 * CLUSTERS * NVEC
    named = (noff_ref[...] * CLUSTERS + nclu_ref[...]).astype(F32).astype(BF16)
    named = jnp.broadcast_to(named, (16, NEAR))
    vec_row = iota((rows, 256), 0) % NVEC == iota((rows, 256), 1) % NVEC
    target_row = (iota((rows, 256), 0) // NVEC).astype(F32)

    def near_sum(g, carry):
        first = g * 16
        spread = (iota((NEAR, 256), 0) == first + iota((NEAR, 256), 1) // NVEC).astype(F32).astype(BF16)
        wanted = jnp.dot(named, spread, preferred_element_type=F32)[0:1, :]
        pick = jnp.where(vec_row & (target_row == wanted), 1.0, 0.0).astype(BF16)
        high = nterm_hi[pl.ds(first, 16)].reshape(256, LEAF)
        low = nterm_lo[pl.ds(first, 16)].reshape(256, LEAF)
        total = jnp.dot(pick, high, preferred_element_type=F32) + jnp.dot(pick, low, preferred_element_type=F32)
        nsum[...] += total.reshape(3 * CLUSTERS, NVEC, LEAF)
        return carry

    def near_piece(q):
        near(2 * q, 0)
        near(2 * q + 1, 0)
        near_sum(q, 0)

    def both_steps(p, carry):
        far_step(p, carry)
        near_piece(p - LAG)
        return merge_step(p - LAG, carry)

    lax.fori_loop(0, LAG, far_step, 0)
    nsum[...] = jnp.zeros_like(nsum)
    lax.fori_loop(LAG, HALF, both_steps, 0)

    def late_steps(p, carry):
        near_piece(p)
        return merge_step(p, carry)

    lax.fori_loop(HALF - LAG, HALF - 1, late_steps, 0)
    near_piece(HALF - 1)
    me = clu * 16 + vol
    before, after = lax.rem(me + NDEV - 1, NDEV), lax.rem(me + 1, NDEV)
    near_copies = []
    for i, (block, to) in enumerate(((0, before), (2, after))):
        copy = pltpu.make_async_remote_copy(
            src_ref=nsum.at[pl.ds(block * CLUSTERS, CLUSTERS)],
            dst_ref=nrecv.at[i],
            send_sem=near_ssem.at[i],
            recv_sem=near_rsem.at[i],
            device_id=(lax.div(to, 16), lax.rem(to, 16)),
            device_id_type=MESH,
        )
        copy.start()
        near_copies.append(copy)

    merge(HALF, HALF - 1)
    total = line_sum(0, HALF - 1) + nsum[pl.ds(CLUSTERS, CLUSTERS)].reshape(CLUSTERS * NVEC, LEAF)
    for copy in near_copies:
        copy.wait()
    total += (nrecv[0] + nrecv[1]).reshape(CLUSTERS * NVEC, LEAF)
    for p in range(HALF):
        for s in (0, HALF):
            if s + p != HALF - 1:
                part = wide_recv.at[s + p]
                pltpu.make_async_copy(part, part, wide_rsem.at[s + p]).wait()
                total += wide_recv[s + p]
    out_ref[...] = total.reshape(CLUSTERS, NVEC, LEAF)

    sent = table.at[pl.ds(0, 240)]
    pltpu.make_async_copy(sent, sent, tab_send).wait()
    sent = ids_recv.at[pl.ds(0, 14)]
    pltpu.make_async_copy(sent, sent, ids_ssem).wait()
    sent = send.at[pl.ds(0, 14)]
    pltpu.make_async_copy(sent, sent, send_sem).wait()
    sent = wide_send.at[pl.ds(0, 15)]
    pltpu.make_async_copy(sent, sent, wide_ssem).wait()


def body(
    volume_field,
    trace_rows,
    near_block,
    near_source,
    near_offset,
    near_cluster,
    far_v,
    far_u,
    far_source,
    far_owner,
    far_cluster,
):
    vmem = pl.BlockSpec(memory_space=pltpu.VMEM)
    hbm = pl.BlockSpec(memory_space=pltpu.HBM)
    dma = pltpu.SemaphoreType.DMA
    return pl.pallas_call(
        kernel,
        out_shape=jax.ShapeDtypeStruct((CLUSTERS, NVEC, LEAF), F32),
        in_specs=[hbm] * 11,
        out_specs=vmem,
        scratch_shapes=[
            pltpu.VMEM((NVEC, TILES // 16 * LEAF), BF16),
            pltpu.SMEM((CLUSTERS, LEAF), jnp.int32),
            pltpu.SMEM((NEAR,), jnp.int32),
            pltpu.VMEM((1, NEAR), jnp.int32),
            pltpu.VMEM((1, NEAR), jnp.int32),
            pltpu.SMEM((FAR,), jnp.int32),
            pltpu.VMEM((1, FAR), jnp.int32),
            pltpu.VMEM((1, FAR), jnp.int32),
            pltpu.VMEM((TILES, NVEC, LEAF), BF16),
            pltpu.VMEM((NEAR, LEAF, LEAF), BF16),
            pltpu.VMEM((FAR, RANK, LEAF), BF16),
            pltpu.VMEM((FAR, RANK, LEAF), BF16),
            pltpu.VMEM((CLUSTERS, NVEC, LEAF), BF16),
            pltpu.VMEM((STEPS, 8, SLOTS * NVEC, LEAF), BF16),
            pltpu.VMEM((STEPS, 8, SLOTS * NVEC, LEAF), BF16),
            pltpu.VMEM((STEPS, LEAF, LEAF), F32),
            pltpu.VMEM((STEPS, LEAF, LEAF), F32),
            pltpu.VMEM((8, NDEV), jnp.int32),
            pltpu.SMEM((8, NDEV), jnp.int32),
            pltpu.VMEM((NDEV, 1, LEAF), F32),
            pltpu.VMEM((STEPS, HALF, 1, LEAF), F32),
            pltpu.VMEM((STEPS, HALF, 1, LEAF), F32),
            pltpu.VMEM((STEPS, LEAF, 8 * SLOTS * NVEC), BF16),
            pltpu.VMEM((NEAR, NVEC, LEAF), BF16),
            pltpu.VMEM((NEAR, NVEC, LEAF), BF16),
            pltpu.VMEM((3 * CLUSTERS, NVEC, LEAF), F32),
            pltpu.VMEM((2, CLUSTERS, NVEC, LEAF), F32),
            dma((11,)),
            dma,
            dma,
            dma((32,)),
            dma,
            dma,
            dma,
            dma((STEPS,)),
            dma,
            dma((STEPS,)),
            dma((2,)),
            dma((2,)),
        ],
        compiler_params=pltpu.CompilerParams(
            collective_id=0, has_side_effects=True, vmem_limit_bytes=40 * 2**20
        ),
        cost_estimate=pl.CostEstimate(flops=2 * 10**8, bytes_accessed=9 * 2**20, transcendentals=0),
    )(
        *(pltpu.with_memory_space_constraint(a, pltpu.HBM) for a in (
        volume_field,
        trace_rows,
        near_source,
        near_offset.reshape(1, NEAR),
        near_cluster.reshape(1, NEAR),
        far_source,
        far_owner.reshape(1, FAR),
        far_cluster.reshape(1, FAR),
        near_block,
        far_v,
        far_u,
    )))


def solution(mesh):
    both = ("clu", "vol")
    return jax.shard_map(
        body,
        mesh=mesh,
        in_specs=(
            P(None, both),
            P(both, None),
            P(both, None, None),
            P(both),
            P(both),
            P(both),
            P(both, None, None),
            P(both, None, None),
            P(both),
            P(both, None),
            P(both),
        ),
        out_specs=P(both, None, None),
        check_vma=False,
    )
```
